128 devices in a mesh: ctx: 32 (over x, z, y_hi), head: 4 (over y_lo, core).
Axes of the slice: x: 4, y: 4 (y_hi: 2, y_lo: 2; y = y_hi * 2 + y_lo), z: 4, core: 2. Of those that a mesh axis runs over, the one named last changes fastest.
Arguments:
- q_win: bfloat16 [8192, 8192], P('ctx', 'head'), may hold values from -64 to 64
- k_win: bfloat16 [8192, 2048], P('ctx', 'head'), may hold values from -6 to 6
- v_win: bfloat16 [8192, 2048], P('ctx', 'head'), may hold values from -5 to 5
- q_lin: bfloat16 [8192, 8192], P('ctx', 'head'), may hold values from -5 to 5
- k_lin: bfloat16 [8192, 2048], P('ctx', 'head'), may hold values from -5 to 5
- v_lin: bfloat16 [8192, 2048], P('ctx', 'head'), may hold values from -5 to 5
- level_table: float32 [64, 64, 6], P(None, 'head'), may hold values from 0.05 to 0.6
- level_index: int32 [8192], P('ctx'), may hold values from 0 to 63
- q_cross: bfloat16 [8192, 8192], P('ctx', 'head'), may hold values from -64 to 64
- k_shared: bfloat16 [8192, 2048], P('ctx', 'head'), may hold values from -6 to 6
- v_shared: bfloat16 [8192, 2048], P('ctx', 'head'), may hold values from -5 to 5
- head_gain: float32 [64], P('head'), may hold values from 0.5 to 13.5
Outputs:
- attended: bfloat16 [8192, 8192], P('ctx', 'head')
The draws below stay inside these ranges and needn't reach their ends.
All inputs are finite; a program needn't handle non-finite values.
Results may differ from the reference program's by a relative error of at most 0.008.
Values may be sent and summed in bfloat16 or wider, within the bound.
A program may use at most 192 MiB of HBM per device.

```python
import math
import jax
import jax.numpy as jnp
import numpy as np
from jax import lax

QH = 64
KVH = 16
HEAD_SIZE = 128
W = 512
TOKENS_PER_SHARD = 256
TABLE = 64
TOKENS = 8192
LEVELS = 6
N_CTX = 32


def drawn_pair(key, salt_value, scale_q):
    base_key = jax.random.fold_in(key, salt_value)
    key_q, key_k = jax.random.split(base_key, 2)
    query_matrix = jnp.clip(jax.random.normal(key_q, (TOKENS, QH, HEAD_SIZE), jnp.float32), -4.0, 4.0) * scale_q
    key_row_slice = jnp.clip(jax.random.normal(key_k, (TOKENS, KVH, HEAD_SIZE), jnp.float32), -4.0, 4.0)
    query_matrix = jnp.clip(query_matrix, -64.0, 64.0).reshape(TOKENS, QH * HEAD_SIZE)
    key_row_slice = jnp.clip(key_row_slice, -6.0, 6.0).reshape(TOKENS, KVH * HEAD_SIZE)
    return (query_matrix, key_row_slice)


def draw_q_win(key, part):
    return drawn_pair(key, 11, 2.5)[0].astype(jnp.bfloat16)


def draw_k_win(key, part):
    return drawn_pair(key, 11, 2.5)[1].astype(jnp.bfloat16)


def draw_q_cross(key, part):
    return drawn_pair(key, 23, 2.5)[0].astype(jnp.bfloat16)


def draw_k_shared(key, part):
    return drawn_pair(key, 23, 2.5)[1].astype(jnp.bfloat16)


def draw_head_gain(key, part):
    base_key = jax.random.fold_in(key, 37)
    spread = jnp.exp(jax.random.uniform(base_key, (QH,), jnp.float32, jnp.log(0.5), jnp.log(1.5)))
    ramp_up = jnp.arange(QH, dtype=jnp.float32) / (QH - 1)
    return spread * 3.0 ** ramp_up


def place_ends(values, rng, smallest, largest):
    extent = values.shape
    index_at = [jax.random.randint(jax.random.fold_in(rng, axis), (), 0, extent[axis]) for axis in range(len(extent))]
    values = values.at[tuple(index_at)].set(smallest)
    longest = extent.index(max(extent))
    index_at[longest] = (index_at[longest] + 1) % extent[longest]
    return values.at[tuple(index_at)].set(largest)


def level_of(own_key, dims, shards, low, top_value):
    def one(position, shards_of):
        steps = jax.random.uniform(jax.random.fold_in(jax.random.fold_in(own_key, 6), position), (shards_of,), jnp.float32, low / len(shards), top_value / len(shards))
        return jnp.repeat(jnp.exp(steps), dims[position] // shards_of).reshape((-1,) + (1,) * (len(dims) - position - 1))

    factor_of = one(*shards[0])
    for cut in shards[1:]:
        factor_of = factor_of * one(*cut)
    return factor_of


def noise(own_key, dims, scale, most, cuts=(), held_as=jnp.bfloat16):
    gain = level_of(own_key, dims, cuts, -0.22, 0.18) if cuts else 1.0
    values = jax.random.normal(own_key, dims, jnp.float32) * scale * gain
    return jnp.minimum(jnp.maximum(values, -most), most).astype(held_as)


def setup_inputs(seed: int = 0) -> dict:
    streams_of = jax.random.split(jax.random.key(seed), 13)
    q_win = draw_q_win(jax.random.fold_in(streams_of[12], 71), 0)
    k_win = draw_k_win(jax.random.fold_in(streams_of[12], 71), 0)
    v_win = noise(streams_of[2], (TOKENS, KVH * HEAD_SIZE), 1.0, 5.0, ((0, 32), (1, 4)))
    q_lin = noise(streams_of[3], (TOKENS, QH * HEAD_SIZE), 1.0, 5.0, ((0, 32), (1, 4)))
    k_lin = noise(streams_of[4], (TOKENS, KVH * HEAD_SIZE), 1.0, 5.0, ((0, 32), (1, 4)))
    v_lin = noise(streams_of[5], (TOKENS, KVH * HEAD_SIZE), 1.0, 5.0, ((0, 32), (1, 4)))
    level_table = jnp.clip(jnp.exp(math.log(0.6) - 2.4849067 * jax.random.uniform(streams_of[6], (TABLE, QH, LEVELS), jnp.float32) ** level_of(streams_of[6], (TABLE, QH, LEVELS), ((1, 4),), -0.2, 0.2)), 0.05, 0.6)
    level_index = place_ends(jax.random.randint(streams_of[7], (TOKENS,), 0, TABLE), jax.random.fold_in(streams_of[7], 1), 0, TABLE - 1).astype(jnp.int32)
    q_cross = draw_q_cross(jax.random.fold_in(streams_of[12], 71), 0)
    k_shared = draw_k_shared(jax.random.fold_in(streams_of[12], 71), 0)
    v_shared = noise(streams_of[10], (TOKENS, KVH * HEAD_SIZE), 1.0, 5.0, ((0, 32), (1, 4)))
    head_gain = draw_head_gain(jax.random.fold_in(streams_of[12], 71), 0)
    return dict(q_win=q_win, k_win=k_win, v_win=v_win, q_lin=q_lin, k_lin=k_lin, v_lin=v_lin, level_table=level_table, level_index=level_index, q_cross=q_cross, k_shared=k_shared, v_shared=v_shared, head_gain=head_gain)


exact_precision_flag = lax.Precision.HIGHEST

def softmax_rows(query_rows, key_row_slice, value_rows, query_pos, key_pos, horizon):
    count_q = query_rows.shape[0]
    count_k = key_row_slice.shape[0]
    per_group = QH // KVH
    allowed = (key_pos[None, :] <= query_pos[:, None]) & (key_pos[None, :] > query_pos[:, None] - horizon)
    query_matrix = query_rows.reshape(count_q, KVH, per_group, HEAD_SIZE).transpose(1, 2, 0, 3).astype(jnp.float32)
    key_heads = key_row_slice.reshape(count_k, KVH, HEAD_SIZE).transpose(1, 0, 2).astype(jnp.float32)
    value_heads = value_rows.reshape(count_k, KVH, HEAD_SIZE).transpose(1, 0, 2).astype(jnp.float32)

    def one_group(members):
        group_q, group_k, group_v = members
        attention_scores = jnp.einsum('rtd,sd->rts', group_q, group_k, precision=exact_precision_flag) * HEAD_SIZE ** (-0.5)
        attention_scores = jnp.where(allowed[None], attention_scores, -1e+30)
        highest = lax.optimization_barrier(jnp.max(attention_scores, axis=-1, keepdims=True))
        weights = jnp.where(allowed[None], jnp.exp(attention_scores - highest), 0.0)
        totals = lax.optimization_barrier(jnp.sum(weights, axis=-1, keepdims=True))
        rounded_values = lax.optimization_barrier(weights.astype(jnp.bfloat16)).astype(jnp.float32)
        return jnp.einsum('rts,sd->rtd', rounded_values, group_v, precision=exact_precision_flag) / totals
    result = lax.map(one_group, (query_matrix, key_heads, value_heads))
    return result.transpose(2, 0, 1, 3).reshape(count_q, QH * HEAD_SIZE)

def causal_pass(query_all, key_all, value_all, horizon):
    block_rows = 512 if TOKENS % 512 == 0 else TOKENS_PER_SHARD
    outputs = []
    for start_row in range(0, TOKENS, block_rows):
        first_key = max(0, start_row - horizon + 1)
        end_row = start_row + block_rows
        outputs.append(softmax_rows(query_all[start_row:end_row], key_all[first_key:end_row], value_all[first_key:end_row], jnp.arange(start_row, end_row, dtype=jnp.int32), jnp.arange(first_key, end_row, dtype=jnp.int32), horizon))
    return jnp.concatenate(outputs, axis=0)

def log_linear(q_lin, k_lin, v_lin, level_table, level_index):
    blocks = N_CTX
    per_group = QH // KVH
    query_matrix = q_lin.reshape(blocks, TOKENS_PER_SHARD, KVH, per_group, HEAD_SIZE).astype(jnp.float32)
    key_blocks = k_lin.reshape(blocks, TOKENS_PER_SHARD, KVH, HEAD_SIZE).astype(jnp.float32)
    value_blocks = v_lin.reshape(blocks, TOKENS_PER_SHARD, KVH, HEAD_SIZE).astype(jnp.float32)
    causal = jnp.arange(TOKENS_PER_SHARD)[:, None] >= jnp.arange(TOKENS_PER_SHARD)[None, :]

    def inner_block(members):
        fenwick_block_query, fenwick_block_key, fenwick_block_value = members
        attention_scores = jnp.einsum('ufjn,efn->fjue', fenwick_block_query, fenwick_block_key, precision=exact_precision_flag) * (HEAD_SIZE * TOKENS_PER_SHARD) ** (-0.5)
        attention_scores = jnp.where(causal, attention_scores, 0.0)
        rounded_values = lax.optimization_barrier(attention_scores.astype(jnp.bfloat16)).astype(jnp.float32)
        return jnp.einsum('koyw,wku->ykou', rounded_values, fenwick_block_value, precision=exact_precision_flag)
    inside = lax.map(inner_block, (query_matrix, key_blocks, value_blocks))
    states = jnp.einsum('nsgd,nsge->ngde', key_blocks, value_blocks, precision=exact_precision_flag)
    level_weights = level_table[level_index].reshape(blocks, TOKENS_PER_SHARD, KVH, per_group, LEVELS)
    mixed_out = level_weights[..., 0:1] * inside
    block_ids = np.arange(blocks)
    for level_no in range(1, LEVELS):
        half_span = 2 ** (level_no - 1)
        grouped = states.reshape(blocks // half_span, half_span, KVH, HEAD_SIZE, HEAD_SIZE).sum(axis=1)
        chosen = np.maximum((block_ids >> level_no - 1) - 1, 0)
        present = block_ids >> level_no - 1 & 1 == 1
        bucket = jnp.where(jnp.asarray(present)[:, None, None, None], grouped[chosen], 0.0)
        readout = jnp.einsum('ntgrd,ngde->ntgre', query_matrix, bucket, precision=exact_precision_flag)
        readout = readout * (HEAD_SIZE * TOKENS_PER_SHARD * half_span) ** (-0.5)
        mixed_out = mixed_out + level_weights[..., level_no:level_no + 1] * readout
    return mixed_out.reshape(TOKENS, QH * HEAD_SIZE)

def reference(q_win, k_win, v_win, q_lin, k_lin, v_lin, level_table, level_index, q_cross, k_shared, v_shared, head_gain):
    window_out = causal_pass(q_win, k_win, v_win, W)
    linear_out = log_linear(q_lin, k_lin, v_lin, level_table, level_index)
    cross_out = causal_pass(q_cross, k_shared, v_shared, TOKENS + 1)
    combined = (window_out + linear_out + cross_out).reshape(TOKENS, QH, HEAD_SIZE) * head_gain[None, :, None]
    mean_square = lax.optimization_barrier(jnp.sum(combined * combined, axis=(1, 2))) / (QH * HEAD_SIZE)
    scaled = combined * lax.rsqrt(mean_square + 1e-06)[:, None, None]
    return scaled.reshape(TOKENS, QH * HEAD_SIZE).astype(jnp.bfloat16)
```

```python
import jax
import jax.numpy as jnp
from jax import lax
from jax.experimental import pallas as pl
from jax.experimental.pallas import tpu as pltpu
from jax.sharding import PartitionSpec as P

bf16 = jnp.bfloat16
f32 = jnp.float32
TOK = 256
D = 128
HEADS = 16
GROUPS = 4
PER = 4
GC = PER * D
LEVELS = 6
W = 512
CTX = 32
NEG = -1e30
EXP2_SCALE = D**-0.5 * 1.4426950408889634


def dot(a, b, ca, cb, precision=None):
    return lax.dot_general(
        a, b, (((ca,), (cb,)), ((), ())), preferred_element_type=f32, precision=precision
    )


def kernel(
    q_win, k_win, v_win, q_lin, k_lin, v_lin, table, index, q_cross, k_sh, v_sh, gain,
    out,
    ql, kl, vl, qw, wk, wv, qb, kb, vb, ob, cr, acc, mx, comb, lw,
    state, fs, fr, hs, hr,
    in_sem, s1s, s1r, ws, wr, qs, qr, fss, frs, zs, zr, bs, br, rs, rr, hss, hrs,
):
    c = lax.axis_index("ctx")
    h = lax.axis_index("head")
    x, z, yh = c // 8, (c // 2) % 4, c % 2
    ylo, core = h // 2, h % 2
    role_head = ylo * 2 + yh
    mixed = core == yh

    def flip(other):
        even = (x + other) % 2 == 0
        return jnp.where(even, z, 3 - z)

    def remote(src, dst, ssem, rsem, cc, hh):
        return pltpu.make_async_remote_copy(
            src_ref=src, dst_ref=dst, send_sem=ssem, recv_sem=rsem,
            device_id=(cc, hh), device_id_type=pl.DeviceIdType.MESH,
        )

    loads = [
        (k_lin, kl), (v_lin, vl), (q_lin, ql), (k_win, wk.at[2]), (v_win, wv.at[2]), (q_win, qw),
    ]
    loads = [pltpu.make_async_copy(s, d, in_sem.at[i]) for i, (s, d) in enumerate(loads)]
    for copy in loads:
        copy.start()

    barrier = pltpu.get_barrier_semaphore()

    def greet(cc, hh):
        pl.semaphore_signal(
            barrier, inc=1, device_id=(cc, hh), device_id_type=pl.DeviceIdType.MESH
        )

    for j in range(4):
        @pl.when(jnp.logical_not(mixed & (x == j)))
        def _():
            greet(j * 8 + z * 2 + core, role_head)
            greet(j * 8 + flip(j) * 2 + core, role_head)
    for dz in range(1, 4):
        greet(x * 8 + (z + dz) % 4 * 2 + yh, h)
        greet(c, (h + dz) % 4)
    for o in (1, 2):
        greet((c + o) % CTX, h)
        greet((c + CTX - o) % CTX, h)
    for level in range(5):
        bit = 2**level
        greet(c + bit - 2 * bit * ((c // bit) % 2), h)
    pl.semaphore_wait(barrier, jnp.where(mixed, 6, 8) + 6 + 4 + 5)

    def s1_copy(j, kv):
        src = (k_sh, v_sh)[kv].at[:, pl.ds(j * D, D)]
        dst = (kb, vb)[kv].at[x, z, pl.ds(yh * TOK, TOK), :]
        return src, dst

    for j in range(4):
        for kv in range(2):
            src, dst = s1_copy(j, kv)
            local = mixed & (x == j)

            @pl.when(local)
            def _():
                pltpu.make_async_copy(src, dst, s1r.at[kv, j]).start()

            @pl.when(jnp.logical_not(local))
            def _():
                remote(
                    src, dst, s1s.at[kv, j], s1r.at[kv, x], j * 8 + z * 2 + core, role_head
                ).start()

    for o in (1, 2):
        for kv in range(2):
            @pl.when(c + o < CTX)
            def _():
                remote(
                    (k_win, v_win)[kv], (wk, wv)[kv].at[2 - o],
                    ws.at[kv, o - 1], wr.at[kv, o - 1], c + o, h,
                ).start()

    for j in range(4):
        src = q_cross.at[:, pl.ds(j * GC, GC)]
        dst = qb.at[x]
        local = mixed & (x == j)

        @pl.when(local)
        def _():
            pltpu.make_async_copy(src, dst, qr.at[j]).start()

        @pl.when(jnp.logical_not(local))
        def _():
            remote(src, dst, qs.at[j], qr.at[x], j * 8 + flip(j) * 2 + core, role_head).start()

    def partner(level):
        bit = 2**level
        return c + bit - 2 * bit * ((c // bit) % 2)

    def f_copy(level):
        return remote(
            fs.at[level], fr.at[level], fss.at[level], frs.at[level], partner(level), h
        )

    def fenwick(level):
        f_copy(level).wait_recv()
        got = fr[level]
        if level < 4:
            total = state[...] + got.astype(f32)
            state[...] = total
            fs[level + 1] = total.astype(bf16)
            f_copy(level + 1).start()

    loads[0].wait()
    loads[1].wait()
    for g in range(GROUPS):
        own = dot(kl[:, g * D : (g + 1) * D], vl[:, g * D : (g + 1) * D], 0, 0)
        state[g] = own
        fs[0, g] = own.astype(bf16)
    f_copy(0).start()

    hot = (lax.broadcasted_iota(jnp.int32, (64, TOK), 0) == index[...]).astype(f32)
    lw[...] = dot(hot, table[...], 0, 0, lax.Precision.HIGHEST)

    loads[2].wait()
    rows = lax.broadcasted_iota(jnp.int32, (TOK, TOK), 0)
    cols = lax.broadcasted_iota(jnp.int32, (TOK, TOK), 1)
    causal = rows >= cols
    for g in range(GROUPS):
        for r in range(PER):
            hd = g * PER + r
            s = dot(ql[:, hd * D : (hd + 1) * D], kl[:, g * D : (g + 1) * D], 1, 1)
            s = jnp.where(causal, s * (D * TOK) ** -0.5, 0.0).astype(bf16)
            comb[:, hd * D : (hd + 1) * D] = lw[:, hd * LEVELS : hd * LEVELS + 1] * dot(
                s, vl[:, g * D : (g + 1) * D], 1, 0
            )

    def z_copy(kv, chunk, dz):
        part = (kb, vb)[kv].at[chunk, z, pl.ds(core * TOK, TOK), :]
        return remote(
            part, part, zs.at[kv, chunk, dz - 1], zr.at[kv, chunk, dz - 1],
            x * 8 + (z + dz) % 4 * 2 + yh, h,
        )

    def z_start(chunk):
        for kv in range(2):
            part = (kb, vb)[kv].at[chunk, z, pl.ds(core * TOK, TOK), :]
            remote(part, part, s1s.at[kv, 0], s1r.at[kv, chunk], c, h).wait_recv()
        for kv in range(2):
            for dz in (1, 3, 2):
                z_copy(kv, chunk, dz).start()

    def b_copy(kv, chunk):
        part = (kb, vb)[kv].at[chunk, :, pl.ds(core * TOK, TOK), :]
        return remote(part, part, bs.at[kv, chunk], br.at[kv, chunk], c, h + 1 - 2 * core)

    def b_start(chunk):
        for kv in range(2):
            for dz in range(1, 4):
                z_copy(kv, chunk, dz).wait_recv()
            b_copy(kv, chunk).start()

    def b_wait(chunk):
        for kv in range(2):
            b_copy(kv, chunk).wait_recv()

    z_start(0)
    fenwick(0)

    for i in (3, 4, 5):
        loads[i].wait()
    for o in (1, 2):
        for kv in range(2):
            ref = (wk, wv)[kv]

            @pl.when(c - o >= 0)
            def _():
                remote(
                    ref.at[2], ref.at[2 - o], ws.at[kv, o - 1], wr.at[kv, o - 1], c, h
                ).wait_recv()

            @pl.when(c - o < 0)
            def _():
                ref[2 - o] = jnp.zeros((TOK, GROUPS * D), bf16)

    far = 3 * TOK
    row = lax.broadcasted_iota(jnp.int32, (TOK, far), 0) + 2 * TOK
    col = lax.broadcasted_iota(jnp.int32, (TOK, far), 1)
    band = (col <= row) & (col > row - W) & (col >= (2 - c) * TOK)
    ones = jnp.ones((far, D), bf16)

    def window_group(g):
        kk = wk[:, :, g * D : (g + 1) * D].reshape(far, D)
        vv = jnp.concatenate([wv[:, :, g * D : (g + 1) * D].reshape(far, D), ones], axis=1)

        def scores(r):
            hd = g * PER + r
            return dot(qw[:, hd * D : (hd + 1) * D], kk, 1, 1)

        nxt = scores(0)
        for r in range(PER):
            s = nxt
            if r + 1 < PER:
                nxt = scores(r + 1)
            hd = g * PER + r
            s = jnp.where(band, s, NEG)
            top = jnp.max(s, axis=1, keepdims=True)
            p = jnp.exp2(s * EXP2_SCALE - top * EXP2_SCALE).astype(bf16)
            o = dot(p, vv, 1, 0)
            comb[:, hd * D : (hd + 1) * D] += o[:, :D] / o[:, D:]

    window_group(0)
    fenwick(1)
    z_start(1)
    window_group(1)
    fenwick(2)
    b_start(0)
    window_group(2)
    fenwick(3)
    z_start(2)
    window_group(3)
    fenwick(4)
    z_start(3)
    b_start(1)

    for level in range(5):
        scale = jnp.where((c // 2**level) % 2 == 1, (D * TOK * 2**level) ** -0.5, 0.0)
        for g in range(GROUPS):
            bucket = fr[level, g]
            for r in range(PER):
                hd = g * PER + r
                term = dot(ql[:, hd * D : (hd + 1) * D], bucket, 1, 0)
                at = hd * LEVELS + level + 1
                comb[:, hd * D : (hd + 1) * D] += (lw[:, at : at + 1] * scale) * term

    acc[...] = jnp.zeros_like(acc)
    mx[...] = jnp.full_like(mx, NEG)
    for j in range(4):
        remote(q_cross.at[:, pl.ds(0, GC)], qb.at[j], qs.at[j], qr.at[j], c, h).wait_recv()

    def attend(blk, kk, vv, mask):
        size = kk.shape[0]
        vv = jnp.concatenate([vv, jnp.ones((size, D), bf16)], axis=1)

        def scores(r):
            return dot(qb[blk, :, r * D : (r + 1) * D], kk, 1, 1)

        nxt = scores(0)
        for r in range(PER):
            s = nxt
            if r + 1 < PER:
                nxt = scores(r + 1)
            if mask is not None:
                s = jnp.where(mask, s, NEG)
            sl = pl.ds(r * TOK, TOK)
            old = mx[blk, sl, :][:, :1]
            new = jnp.maximum(old, jnp.max(s, axis=1, keepdims=True))
            p = jnp.exp2(s * EXP2_SCALE - new * EXP2_SCALE).astype(bf16)
            damp = jnp.exp2((old - new) * EXP2_SCALE)
            acc[blk, sl, :] = acc[blk, sl, :] * damp + dot(p, vv, 1, 0)
            mx[blk, sl, :] = jnp.broadcast_to(new, (TOK, D))

    half = 1024

    def half_kv(ref, chunk, part):
        return ref[chunk, pl.ds(part * 2, 2)].reshape(half, D)

    def r_copy(blk):
        return remote(
            ob.at[blk], cr.at[x], rs.at[blk], rr.at[x],
            blk * 8 + flip(blk) * 2 + core, role_head,
        )

    def chunk_step(chunk, carry):
        b_wait(chunk)

        @pl.when(chunk < 3)
        def _():
            @pl.when(chunk > 0)
            def _():
                b_start(chunk + 1)

        place = flip(chunk) * 2 + core

        def full_half(part, carry2):
            attend(chunk, half_kv(kb, chunk, part), half_kv(vb, chunk, part), None)
            return carry2

        lax.fori_loop(0, place // 4, full_half, 0)
        part = place // 4
        first = (place % 4) * TOK
        row = lax.broadcasted_iota(jnp.int32, (TOK, half), 0) + first
        col = lax.broadcasted_iota(jnp.int32, (TOK, half), 1)
        attend(chunk, half_kv(kb, chunk, part), half_kv(vb, chunk, part), col <= row)
        for r in range(PER):
            sl = pl.ds(r * TOK, TOK)
            ob[chunk, :, r * D : (r + 1) * D] = (
                acc[chunk, sl, :D] / acc[chunk, sl, D:]
            ).astype(bf16)
        local = mixed & (x == chunk)

        @pl.when(local)
        def _():
            pltpu.make_async_copy(ob.at[chunk], cr.at[x], rr.at[x]).start()

        @pl.when(jnp.logical_not(local))
        def _():
            r_copy(chunk).start()

        def full(blk, carry2):
            attend(blk, kb[chunk].reshape(2048, D), vb[chunk].reshape(2048, D), None)
            return carry2

        lax.fori_loop(chunk + 1, 4, full, 0)
        return carry

    lax.fori_loop(0, 4, chunk_step, 0)

    square = jnp.zeros((TOK, D), f32)
    for j in range(4):
        remote(ob.at[j], cr.at[j], rs.at[j], rr.at[j], c, h).wait_recv()
        for r in range(PER):
            hd = j * PER + r
            at = slice(hd * D, (hd + 1) * D)
            v = (comb[:, at] + cr[j, :, r * D : (r + 1) * D].astype(f32)) * gain[hd]
            comb[:, at] = v
            square += v * v
    hs[...] = dot(jnp.ones((8, D), f32), square, 1, 1, lax.Precision.HIGHEST)
    for d in range(1, 4):
        remote(hs, hr.at[d - 1], hss.at[d - 1], hrs.at[d - 1], c, (h + d) % 4).start()
    total = hs[...]
    for d in range(1, 4):
        remote(hs, hr.at[d - 1], hss.at[d - 1], hrs.at[d - 1], c, (h + d) % 4).wait_recv()
        total = total + hr[d - 1]
    norm = lax.rsqrt(total / (4 * HEADS * D) + 1e-6).T[:, :1]
    for hd in range(HEADS):
        at = slice(hd * D, (hd + 1) * D)
        out[:, at] = (comb[:, at] * norm).astype(bf16)

    for j in range(4):
        local = mixed & (x == j)

        @pl.when(jnp.logical_not(local))
        def _():
            for kv in range(2):
                src, dst = s1_copy(j, kv)
                remote(src, dst, s1s.at[kv, j], s1r.at[kv, x], c, h).wait_send()
            remote(
                q_cross.at[:, pl.ds(j * GC, GC)], qb.at[x], qs.at[j], qr.at[x], c, h
            ).wait_send()
            r_copy(j).wait_send()
        for kv in range(2):
            b_copy(kv, j).wait_send()
            for dz in range(1, 4):
                z_copy(kv, j, dz).wait_send()
    for o in (1, 2):
        for kv in range(2):
            @pl.when(c + o < CTX)
            def _():
                remote(
                    (k_win, v_win)[kv], (wk, wv)[kv].at[2 - o],
                    ws.at[kv, o - 1], wr.at[kv, o - 1], c, h,
                ).wait_send()
    for level in range(5):
        f_copy(level).wait_send()
    for d in range(1, 4):
        remote(hs, hr.at[d - 1], hss.at[d - 1], hrs.at[d - 1], c, h).wait_send()


def per_device(
    q_win, k_win, v_win, q_lin, k_lin, v_lin, level_table, level_index, q_cross, k_shared,
    v_shared, head_gain,
):
    dma = pltpu.SemaphoreType.DMA
    whole = pl.BlockSpec(memory_space=pl.ANY)
    vmem = pl.BlockSpec(memory_space=pltpu.VMEM)
    smem = pl.BlockSpec(memory_space=pltpu.SMEM)
    kv = GROUPS * D
    return pl.pallas_call(
        kernel,
        out_shape=jax.ShapeDtypeStruct((TOK, HEADS * D), bf16),
        in_specs=[whole] * 6 + [vmem, vmem] + [whole] * 3 + [smem],
        out_specs=vmem,
        scratch_shapes=[
            pltpu.VMEM((TOK, HEADS * D), bf16),
            pltpu.VMEM((TOK, kv), bf16),
            pltpu.VMEM((TOK, kv), bf16),
            pltpu.VMEM((TOK, HEADS * D), bf16),
            pltpu.VMEM((3, TOK, kv), bf16),
            pltpu.VMEM((3, TOK, kv), bf16),
            pltpu.VMEM((4, TOK, GC), bf16),
            pltpu.VMEM((4, 4, 2 * TOK, D), bf16),
            pltpu.VMEM((4, 4, 2 * TOK, D), bf16),
            pltpu.VMEM((4, TOK, GC), bf16),
            pltpu.VMEM((4, TOK, GC), bf16),
            pltpu.VMEM((4, PER * TOK, 2 * D), f32),
            pltpu.VMEM((4, PER * TOK, D), f32),
            pltpu.VMEM((TOK, HEADS * D), f32),
            pltpu.VMEM((TOK, HEADS * LEVELS), f32),
            pltpu.VMEM((GROUPS, D, D), f32),
            pltpu.VMEM((5, GROUPS, D, D), bf16),
            pltpu.VMEM((5, GROUPS, D, D), bf16),
            pltpu.VMEM((8, TOK), f32),
            pltpu.VMEM((3, 8, TOK), f32),
            dma((6,)),
            dma((2, 4)), dma((2, 4)),
            dma((2, 2)), dma((2, 2)),
            dma((4,)), dma((4,)),
            dma((5,)), dma((5,)),
            dma((2, 4, 3)), dma((2, 4, 3)),
            dma((2, 4)), dma((2, 4)),
            dma((4,)), dma((4,)),
            dma((3,)), dma((3,)),
        ],
        compiler_params=pltpu.CompilerParams(
            collective_id=0, has_side_effects=True, vmem_limit_bytes=56 * 2**20
        ),
        name="hybrid_attention",
    )(
        q_win, k_win, v_win, q_lin, k_lin, v_lin,
        level_table.reshape(level_table.shape[0], -1), level_index.reshape(1, -1),
        q_cross, k_shared, v_shared, head_gain,
    )


def solution(mesh):
    return jax.shard_map(
        per_device,
        mesh=mesh,
        in_specs=(
            P("ctx", "head"),
            P("ctx", "head"),
            P("ctx", "head"),
            P("ctx", "head"),
            P("ctx", "head"),
            P("ctx", "head"),
            P(None, "head", None),
            P("ctx"),
            P("ctx", "head"),
            P("ctx", "head"),
            P("ctx", "head"),
            P("head"),
        ),
        out_specs=P("ctx", "head"),
        check_vma=False,
    )
```

```python
import jax
import jax.numpy as jnp
from jax import lax
from jax.experimental import pallas as pl
from jax.experimental.pallas import tpu as pltpu
from jax.sharding import PartitionSpec as P

bf16 = jnp.bfloat16
f32 = jnp.float32
TOK = 256
D = 128
HEADS = 16
GROUPS = 4
PER = 4
GC = PER * D
LEVELS = 6
W = 512
CTX = 32
NEG = -1e30
EXP2_SCALE = D**-0.5 * 1.4426950408889634


def dot(a, b, ca, cb, precision=None):
    return lax.dot_general(
        a, b, (((ca,), (cb,)), ((), ())), preferred_element_type=f32, precision=precision
    )


def kernel(
    q_win, k_win, v_win, q_lin, k_lin, v_lin, table, index, q_cross, k_sh, v_sh, gain,
    out,
    ql, kl, vl, qw, wk, wv, qb, kb, vb, ob, cr, acc, mx, comb, lw,
    state, fs, fr, hs, hr,
    in_sem, s1s, s1r, ws, wr, qs, qr, fss, frs, zs, zr, bs, br, rs, rr, hss, hrs,
):
    c = lax.axis_index("ctx")
    h = lax.axis_index("head")
    x, z, yh = c // 8, (c // 2) % 4, c % 2
    ylo, core = h // 2, h % 2
    role_head = ylo * 2 + yh
    mixed = core == yh

    def remote(src, dst, ssem, rsem, cc, hh):
        return pltpu.make_async_remote_copy(
            src_ref=src, dst_ref=dst, send_sem=ssem, recv_sem=rsem,
            device_id=(cc, hh), device_id_type=pl.DeviceIdType.MESH,
        )

    loads = [
        (k_lin, kl), (v_lin, vl), (q_lin, ql), (k_win, wk.at[2]), (v_win, wv.at[2]), (q_win, qw),
    ]
    loads = [pltpu.make_async_copy(s, d, in_sem.at[i]) for i, (s, d) in enumerate(loads)]
    for copy in loads:
        copy.start()

    barrier = pltpu.get_barrier_semaphore()

    def greet(cc, hh):
        pl.semaphore_signal(
            barrier, inc=1, device_id=(cc, hh), device_id_type=pl.DeviceIdType.MESH
        )

    def partner(level):
        bit = 2**level
        return c + bit - 2 * bit * ((c // bit) % 2)

    for j in range(4):
        @pl.when(jnp.logical_not(mixed & (x == j)))
        def _():
            greet(j * 8 + z * 2 + core, role_head)

    @pl.when(jnp.logical_not(mixed))
    def _():
        greet(partner(3), h)
        greet(partner(4), h)

    for dz in range(1, 4):
        greet(x * 8 + (z + dz) % 4 * 2 + yh, h)
        greet(c, (h + dz) % 4)
    greet(partner(0), h)

    @pl.when(z == 3)
    def _():
        greet((c + 2) % CTX, h)

    @pl.when(z == 0)
    def _():
        greet((c + CTX - 2) % CTX, h)

    loads[0].wait()
    loads[1].wait()
    for g in range(GROUPS):
        own = dot(kl[:, g * D : (g + 1) * D], vl[:, g * D : (g + 1) * D], 0, 0)
        state[g] = own
        fs[0, g] = own.astype(bf16)

    hot = (lax.broadcasted_iota(jnp.int32, (64, TOK), 0) == index[...]).astype(f32)
    lw[...] = dot(hot, table[...], 0, 0, lax.Precision.HIGHEST)

    loads[2].wait()
    rows = lax.broadcasted_iota(jnp.int32, (TOK, TOK), 0)
    cols = lax.broadcasted_iota(jnp.int32, (TOK, TOK), 1)
    causal = rows >= cols
    for g in range(GROUPS):
        for r in range(PER):
            hd = g * PER + r
            s = dot(ql[:, hd * D : (hd + 1) * D], kl[:, g * D : (g + 1) * D], 1, 1)
            s = jnp.where(causal, s * (D * TOK) ** -0.5, 0.0).astype(bf16)
            comb[:, hd * D : (hd + 1) * D] = lw[:, hd * LEVELS : hd * LEVELS + 1] * dot(
                s, vl[:, g * D : (g + 1) * D], 1, 0
            )

    pl.semaphore_wait(
        barrier,
        jnp.where(mixed, 3, 6) + 7 + jnp.where((z == 0) | (z == 3), 1, 0),
    )

    def s1_copy(j, kv):
        src = (k_sh, v_sh)[kv].at[:, pl.ds(j * D, D)]
        dst = (kb, vb)[kv].at[x, z, pl.ds(yh * TOK, TOK), :]
        return src, dst

    for j in range(4):
        for kv in range(2):
            src, dst = s1_copy(j, kv)
            local = mixed & (x == j)

            @pl.when(local)
            def _():
                pltpu.make_async_copy(src, dst, s1r.at[kv, j]).start()

            @pl.when(jnp.logical_not(local))
            def _():
                remote(
                    src, dst, s1s.at[kv, j], s1r.at[kv, x], j * 8 + z * 2 + core, role_head
                ).start()

    def f_copy(level):
        return remote(
            fs.at[level], fr.at[level], fss.at[level], frs.at[level], partner(level), h
        )

    def fenwick(level):
        f_copy(level).wait_recv()
        got = fr[level]
        if level < 4:
            total = state[...] + got.astype(f32)
            state[...] = total
            fs[level + 1] = total.astype(bf16)
            f_copy(level + 1).start()

    f_copy(0).start()

    for j in range(4):
        src = q_cross.at[:, pl.ds(j * GC, GC)]
        dst = qb.at[x]
        local = mixed & (x == j)

        @pl.when(local)
        def _():
            pltpu.make_async_copy(src, dst, qr.at[j]).start()

        @pl.when(jnp.logical_not(local))
        def _():
            remote(src, dst, qs.at[j], qr.at[x], j * 8 + z * 2 + core, role_head).start()

    def z_copy(kv, chunk, step):
        tile = (z + 1) % 4 if step == 2 else z
        to = (z + 1) % 4 if step == 0 else (z + 3) % 4
        part = (kb, vb)[kv].at[chunk, tile, pl.ds(core * TOK, TOK), :]
        return remote(
            part, part, zs.at[kv, chunk, step], zr.at[kv, chunk, step],
            x * 8 + to * 2 + yh, h,
        )

    def z_start(chunk):
        for kv in range(2):
            part = (kb, vb)[kv].at[chunk, z, pl.ds(core * TOK, TOK), :]
            remote(part, part, s1s.at[kv, 0], s1r.at[kv, chunk], c, h).wait_recv()
            for step in (1, 0):
                z_copy(kv, chunk, step).start()

    def z_forward(chunk):
        for kv in range(2):
            z_copy(kv, chunk, 1).wait_recv()
            z_copy(kv, chunk, 2).start()

    def b_copy(kv, chunk):
        part = (kb, vb)[kv].at[chunk, :, pl.ds(core * TOK, TOK), :]
        return remote(part, part, bs.at[kv, chunk], br.at[kv, chunk], c, h + 1 - 2 * core)

    def b_start(chunk):
        for kv in range(2):
            for step in (0, 2):
                z_copy(kv, chunk, step).wait_recv()
            b_copy(kv, chunk).start()

    def b_wait(chunk):
        for kv in range(2):
            b_copy(kv, chunk).wait_recv()

    def w_copy(kv):
        return remote(
            (k_win, v_win)[kv], (wk, wv)[kv].at[0], ws.at[kv, 0], wr.at[kv, 0], c + 2, h
        )

    def w_start():
        for kv in range(2):
            @pl.when(c + 2 < CTX)
            def _():
                w_copy(kv).start()

    def y_copy(kv, slot):
        ref = (wk, wv)[kv]
        return remote(ref.at[slot], ref.at[1], ws.at[kv, 1], wr.at[kv, 1], partner(0), h)

    def w_arrive():
        for kv in range(2):
            ref = (wk, wv)[kv]

            @pl.when(c >= 2)
            def _():
                w_copy(kv).wait_recv()

            @pl.when(c < 2)
            def _():
                ref[0] = jnp.zeros((TOK, GROUPS * D), bf16)

            @pl.when(yh == 1)
            def _():
                y_copy(kv, 0).start()

    z_start(0)
    for i in (3, 4, 5):
        loads[i].wait()
    for kv in range(2):
        @pl.when(yh == 0)
        def _():
            y_copy(kv, 2).start()
    z_start(1)
    z_forward(0)
    w_start()

    b_start(0)

    acc[...] = jnp.zeros_like(acc)
    mx[...] = jnp.full_like(mx, NEG)
    for j in range(4):
        remote(q_cross.at[:, pl.ds(0, GC)], qb.at[j], qs.at[j], qr.at[j], c, h).wait_recv()

    def attend(blk, kk, vv, mask):
        size = kk.shape[0]
        vv = jnp.concatenate([vv, jnp.ones((size, D), bf16)], axis=1)

        def scores(r):
            return dot(qb[blk, :, r * D : (r + 1) * D], kk, 1, 1)

        nxt = scores(0)
        for r in range(PER):
            s = nxt
            if r + 1 < PER:
                nxt = scores(r + 1)
            if mask is not None:
                s = jnp.where(mask, s, NEG)
            sl = pl.ds(r * TOK, TOK)
            old = mx[blk, sl, :][:, :1]
            new = jnp.maximum(old, jnp.max(s, axis=1, keepdims=True))
            p = jnp.exp2(s * EXP2_SCALE - new * EXP2_SCALE).astype(bf16)
            damp = jnp.exp2((old - new) * EXP2_SCALE)
            acc[blk, sl, :] = acc[blk, sl, :] * damp + dot(p, vv, 1, 0)
            mx[blk, sl, :] = jnp.broadcast_to(new, (TOK, D))

    half = 1024

    def half_kv(ref, chunk, part):
        return ref[chunk, pl.ds(part * 2, 2)].reshape(half, D)

    def r_copy(blk):
        return remote(
            ob.at[blk], cr.at[x], rs.at[blk], rr.at[x],
            blk * 8 + z * 2 + core, role_head,
        )

    place = z * 2 + core

    def chunk_step(chunk, carry):
        b_wait(chunk)

        def masked(size, kk, vv):
            row = lax.broadcasted_iota(jnp.int32, (TOK, size), 0) + place * TOK
            col = lax.broadcasted_iota(jnp.int32, (TOK, size), 1)
            attend(chunk, kk, vv, col <= row)

        @pl.when(z < 2)
        def _():
            masked(half, half_kv(kb, chunk, 0), half_kv(vb, chunk, 0))

        @pl.when(z >= 2)
        def _():
            masked(2048, kb[chunk].reshape(2048, D), vb[chunk].reshape(2048, D))

        for r in range(PER):
            sl = pl.ds(r * TOK, TOK)
            ob[chunk, :, r * D : (r + 1) * D] = (
                acc[chunk, sl, :D] / acc[chunk, sl, D:]
            ).astype(bf16)
        local = mixed & (x == chunk)

        @pl.when(local)
        def _():
            pltpu.make_async_copy(ob.at[chunk], cr.at[x], rr.at[x]).start()

        @pl.when(jnp.logical_not(local))
        def _():
            r_copy(chunk).start()

        @pl.when(chunk == 0)
        def _():
            fenwick(0)
            z_start(2)
            z_forward(1)

        @pl.when(chunk == 1)
        def _():
            b_start(2)
            fenwick(4)

        @pl.when(chunk == 2)
        def _():
            b_start(3)

        def full(blk, carry2):
            @pl.when((chunk == 0) & (blk == 1))
            def _():
                fenwick(1)
                z_start(3)
                b_start(1)

            @pl.when((chunk == 0) & (blk == 2))
            def _():
                fenwick(2)
                z_forward(2)

            @pl.when((chunk == 0) & (blk == 3))
            def _():
                fenwick(3)
                z_forward(3)
                w_arrive()

            attend(blk, kb[chunk].reshape(2048, D), vb[chunk].reshape(2048, D), None)
            return carry2

        lax.fori_loop(chunk + 1, 4, full, 0)
        return carry

    lax.fori_loop(0, 4, chunk_step, 0)

    for level in range(5):
        scale = jnp.where((c // 2**level) % 2 == 1, (D * TOK * 2**level) ** -0.5, 0.0)
        for g in range(GROUPS):
            bucket = fr[level, g]
            for r in range(PER):
                hd = g * PER + r
                term = dot(ql[:, hd * D : (hd + 1) * D], bucket, 1, 0)
                at = hd * LEVELS + level + 1
                comb[:, hd * D : (hd + 1) * D] += (lw[:, at : at + 1] * scale) * term

    for kv in range(2):
        y_copy(kv, 0).wait_recv()

    far = 3 * TOK
    row = lax.broadcasted_iota(jnp.int32, (TOK, far), 0) + 2 * TOK
    col = lax.broadcasted_iota(jnp.int32, (TOK, far), 1)
    band = (col <= row) & (col > row - W) & (col >= (2 - c) * TOK)
    ones = jnp.ones((far, D), bf16)

    def window_group(g):
        kk = wk[:, :, g * D : (g + 1) * D].reshape(far, D)
        vv = jnp.concatenate([wv[:, :, g * D : (g + 1) * D].reshape(far, D), ones], axis=1)

        def scores(r):
            hd = g * PER + r
            return dot(qw[:, hd * D : (hd + 1) * D], kk, 1, 1)

        nxt = scores(0)
        for r in range(PER):
            s = nxt
            if r + 1 < PER:
                nxt = scores(r + 1)
            hd = g * PER + r
            s = jnp.where(band, s, NEG)
            top = jnp.max(s, axis=1, keepdims=True)
            p = jnp.exp2(s * EXP2_SCALE - top * EXP2_SCALE).astype(bf16)
            o = dot(p, vv, 1, 0)
            comb[:, hd * D : (hd + 1) * D] += o[:, :D] / o[:, D:]

    for g in range(GROUPS):
        window_group(g)


    square = jnp.zeros((TOK, D), f32)
    for j in range(4):
        remote(ob.at[j], cr.at[j], rs.at[j], rr.at[j], c, h).wait_recv()
        for r in range(PER):
            hd = j * PER + r
            at = slice(hd * D, (hd + 1) * D)
            v = (comb[:, at] + cr[j, :, r * D : (r + 1) * D].astype(f32)) * gain[hd]
            comb[:, at] = v
            square += v * v
    hs[...] = dot(jnp.ones((8, D), f32), square, 1, 1, lax.Precision.HIGHEST)
    for d in range(1, 4):
        remote(hs, hr.at[d - 1], hss.at[d - 1], hrs.at[d - 1], c, (h + d) % 4).start()
    total = hs[...]
    for d in range(1, 4):
        remote(hs, hr.at[d - 1], hss.at[d - 1], hrs.at[d - 1], c, (h + d) % 4).wait_recv()
        total = total + hr[d - 1]
    norm = lax.rsqrt(total / (4 * HEADS * D) + 1e-6).T[:, :1]
    for hd in range(HEADS):
        at = slice(hd * D, (hd + 1) * D)
        out[:, at] = (comb[:, at] * norm).astype(bf16)

    for j in range(4):
        local = mixed & (x == j)

        @pl.when(jnp.logical_not(local))
        def _():
            for kv in range(2):
                src, dst = s1_copy(j, kv)
                remote(src, dst, s1s.at[kv, j], s1r.at[kv, x], c, h).wait_send()
            remote(
                q_cross.at[:, pl.ds(j * GC, GC)], qb.at[x], qs.at[j], qr.at[x], c, h
            ).wait_send()
            r_copy(j).wait_send()
        for kv in range(2):
            b_copy(kv, j).wait_send()
            for step in range(3):
                z_copy(kv, j, step).wait_send()
    for kv in range(2):
        y_copy(kv, 0).wait_send()

        @pl.when(c + 2 < CTX)
        def _():
            w_copy(kv).wait_send()
    for level in range(5):
        f_copy(level).wait_send()
    for d in range(1, 4):
        remote(hs, hr.at[d - 1], hss.at[d - 1], hrs.at[d - 1], c, h).wait_send()


def per_device(
    q_win, k_win, v_win, q_lin, k_lin, v_lin, level_table, level_index, q_cross, k_shared,
    v_shared, head_gain,
):
    dma = pltpu.SemaphoreType.DMA
    whole = pl.BlockSpec(memory_space=pl.ANY)
    vmem = pl.BlockSpec(memory_space=pltpu.VMEM)
    smem = pl.BlockSpec(memory_space=pltpu.SMEM)
    kv = GROUPS * D
    return pl.pallas_call(
        kernel,
        out_shape=jax.ShapeDtypeStruct((TOK, HEADS * D), bf16),
        in_specs=[whole] * 6 + [vmem, vmem] + [whole] * 3 + [smem],
        out_specs=vmem,
        scratch_shapes=[
            pltpu.VMEM((TOK, HEADS * D), bf16),
            pltpu.VMEM((TOK, kv), bf16),
            pltpu.VMEM((TOK, kv), bf16),
            pltpu.VMEM((TOK, HEADS * D), bf16),
            pltpu.VMEM((3, TOK, kv), bf16),
            pltpu.VMEM((3, TOK, kv), bf16),
            pltpu.VMEM((4, TOK, GC), bf16),
            pltpu.VMEM((4, 4, 2 * TOK, D), bf16),
            pltpu.VMEM((4, 4, 2 * TOK, D), bf16),
            pltpu.VMEM((4, TOK, GC), bf16),
            pltpu.VMEM((4, TOK, GC), bf16),
            pltpu.VMEM((4, PER * TOK, 2 * D), f32),
            pltpu.VMEM((4, PER * TOK, D), f32),
            pltpu.VMEM((TOK, HEADS * D), f32),
            pltpu.VMEM((TOK, HEADS * LEVELS), f32),
            pltpu.VMEM((GROUPS, D, D), f32),
            pltpu.VMEM((5, GROUPS, D, D), bf16),
            pltpu.VMEM((5, GROUPS, D, D), bf16),
            pltpu.VMEM((8, TOK), f32),
            pltpu.VMEM((3, 8, TOK), f32),
            dma((6,)),
            dma((2, 4)), dma((2, 4)),
            dma((2, 2)), dma((2, 2)),
            dma((4,)), dma((4,)),
            dma((5,)), dma((5,)),
            dma((2, 4, 3)), dma((2, 4, 3)),
            dma((2, 4)), dma((2, 4)),
            dma((4,)), dma((4,)),
            dma((3,)), dma((3,)),
        ],
        compiler_params=pltpu.CompilerParams(
            collective_id=0, has_side_effects=True, vmem_limit_bytes=56 * 2**20
        ),
        name="hybrid_attention",
    )(
        q_win, k_win, v_win, q_lin, k_lin, v_lin,
        level_table.reshape(level_table.shape[0], -1), level_index.reshape(1, -1),
        q_cross, k_shared, v_shared, head_gain,
    )


def solution(mesh):
    return jax.shard_map(
        per_device,
        mesh=mesh,
        in_specs=(
            P("ctx", "head"),
            P("ctx", "head"),
            P("ctx", "head"),
            P("ctx", "head"),
            P("ctx", "head"),
            P("ctx", "head"),
            P(None, "head", None),
            P("ctx"),
            P("ctx", "head"),
            P("ctx", "head"),
            P("ctx", "head"),
            P("head"),
        ),
        out_specs=P("ctx", "head"),
        check_vma=False,
    )
```

```python
import jax
import jax.numpy as jnp
from jax import lax
from jax.experimental import pallas as pl
from jax.experimental.pallas import tpu as pltpu
from jax.sharding import PartitionSpec as P

bf16 = jnp.bfloat16
f32 = jnp.float32
TOK = 256
D = 128
HEADS = 16
GROUPS = 4
PER = 4
GC = PER * D
LEVELS = 6
W = 512
CTX = 32
NEG = -1e30
EXP2_SCALE = D**-0.5 * 1.4426950408889634


def dot(a, b, ca, cb, precision=None):
    return lax.dot_general(
        a, b, (((ca,), (cb,)), ((), ())), preferred_element_type=f32, precision=precision
    )


def kernel(
    q_win, k_win, v_win, q_lin, k_lin, v_lin, table, index, q_cross, k_sh, v_sh, gain,
    out,
    ql, kl, vl, qw, wk, wv, qb, kb, vb, ob, cr, acc, mx, comb, lw,
    state, fs, fr, hs, hr,
    in_sem, s1s, s1r, ws, wr, qs, qr, fss, frs, zs, zr, bs, br, rs, rr, hss, hrs,
):
    c = lax.axis_index("ctx")
    h = lax.axis_index("head")
    x, z, yh = c // 8, (c // 2) % 4, c % 2
    ylo, core = h // 2, h % 2
    role_head = ylo * 2 + yh
    mixed = core == yh

    def remote(src, dst, ssem, rsem, cc, hh):
        return pltpu.make_async_remote_copy(
            src_ref=src, dst_ref=dst, send_sem=ssem, recv_sem=rsem,
            device_id=(cc, hh), device_id_type=pl.DeviceIdType.MESH,
        )

    loads = [
        (k_lin, kl), (v_lin, vl), (q_lin, ql), (k_win, wk.at[2]), (v_win, wv.at[2]), (q_win, qw),
    ]
    loads = [pltpu.make_async_copy(s, d, in_sem.at[i]) for i, (s, d) in enumerate(loads)]
    for copy in loads:
        copy.start()

    barrier = pltpu.get_barrier_semaphore()

    def greet(cc, hh):
        pl.semaphore_signal(
            barrier, inc=1, device_id=(cc, hh), device_id_type=pl.DeviceIdType.MESH
        )

    def partner(level):
        bit = 2**level
        return c + bit - 2 * bit * ((c // bit) % 2)

    for j in range(4):
        @pl.when(jnp.logical_not(mixed & (x == j)))
        def _():
            greet(j * 8 + z * 2 + core, role_head)

    @pl.when(jnp.logical_not(mixed))
    def _():
        greet(partner(3), h)
        greet(partner(4), h)

    for dz in range(1, 4):
        greet(x * 8 + (z + dz) % 4 * 2 + yh, h)
        greet(c, (h + dz) % 4)
    greet(partner(0), h)

    @pl.when(z == 3)
    def _():
        greet((c + 2) % CTX, h)

    @pl.when(z == 0)
    def _():
        greet((c + CTX - 2) % CTX, h)

    loads[0].wait()
    loads[1].wait()
    for g in range(GROUPS):
        own = dot(kl[:, g * D : (g + 1) * D], vl[:, g * D : (g + 1) * D], 0, 0)
        state[g] = own
        fs[0, g] = own.astype(bf16)

    hot = (lax.broadcasted_iota(jnp.int32, (64, TOK), 0) == index[...]).astype(f32)
    lw[...] = dot(hot, table[...], 0, 0, lax.Precision.HIGHEST)

    loads[2].wait()
    rows = lax.broadcasted_iota(jnp.int32, (TOK, TOK), 0)
    cols = lax.broadcasted_iota(jnp.int32, (TOK, TOK), 1)
    causal = rows >= cols
    for g in range(GROUPS):
        for r in range(PER):
            hd = g * PER + r
            s = dot(ql[:, hd * D : (hd + 1) * D], kl[:, g * D : (g + 1) * D], 1, 1)
            s = jnp.where(causal, s * (D * TOK) ** -0.5, 0.0).astype(bf16)
            comb[:, hd * D : (hd + 1) * D] = lw[:, hd * LEVELS : hd * LEVELS + 1] * dot(
                s, vl[:, g * D : (g + 1) * D], 1, 0
            )

    pl.semaphore_wait(
        barrier,
        jnp.where(mixed, 3, 6) + 7 + jnp.where((z == 0) | (z == 3), 1, 0),
    )

    def s1_copy(j, kv):
        src = (k_sh, v_sh)[kv].at[:, pl.ds(j * D, D)]
        dst = (kb, vb)[kv].at[z, x, pl.ds(yh * TOK, TOK), :]
        return src, dst

    def f_copy(level):
        return remote(
            fs.at[level], fr.at[level], fss.at[level], frs.at[level], partner(level), h
        )

    def fenwick(level):
        f_copy(level).wait_recv()
        got = fr[level]
        if level < 4:
            total = state[...] + got.astype(f32)
            state[...] = total
            fs[level + 1] = total.astype(bf16)
            f_copy(level + 1).start()

    f_copy(0).start()

    for j in range(4):
        for kv in range(2):
            src, dst = s1_copy(j, kv)
            local = mixed & (x == j)

            @pl.when(local)
            def _():
                pltpu.make_async_copy(src, dst, s1r.at[kv, j]).start()

            @pl.when(jnp.logical_not(local))
            def _():
                remote(
                    src, dst, s1s.at[kv, j], s1r.at[kv, x], j * 8 + z * 2 + core, role_head
                ).start()

    def q_copy(t):
        j = (x + 4 - t) % 4
        return (
            q_cross.at[:, pl.ds(j * GC, GC)], qb.at[x], qs.at[t], qr.at[x],
            j * 8 + z * 2 + core, role_head,
        )

    def q_start(t):
        src, dst, ssem, rsem, cc, hh = q_copy(t)
        if t == 0:
            @pl.when(mixed)
            def _():
                pltpu.make_async_copy(src, dst, rsem).start()

            @pl.when(jnp.logical_not(mixed))
            def _():
                remote(src, dst, ssem, rsem, cc, hh).start()
        else:
            remote(src, dst, ssem, rsem, cc, hh).start()

    def z_copy(kv, step):
        if step == 2:
            tile, to = ((z + 1) % 4, (z + 3) % 4) if kv == 0 else ((z + 3) % 4, (z + 1) % 4)
        else:
            tile, to = z, (z + 1 + 2 * step) % 4
        part = (kb, vb)[kv].at[tile, :, pl.ds(core * TOK, TOK), :]
        return remote(
            part, part, zs.at[kv, step], zr.at[kv, step], x * 8 + to * 2 + yh, h
        )

    def z_of(n):
        return (z + jnp.where(n == 1, 3, jnp.where(n == 2, 1, jnp.where(n == 3, 2, 0)))) % 4

    def b_copy(kv, n):
        part = (kb, vb)[kv].at[z_of(n), :, pl.ds(core * TOK, TOK), :]
        return remote(part, part, bs.at[kv, n], br.at[kv, n], c, h + 1 - 2 * core)

    def b_start(n):
        for kv in range(2):
            if n > 0:
                z_copy(kv, n - 1).wait_recv()
            b_copy(kv, n).start()
        if n == 1:
            z_copy(1, 2).start()
        if n == 2:
            z_copy(0, 2).start()

    def b_wait(n):
        for kv in range(2):
            b_copy(kv, n).wait_recv()

    def own_chunk():
        for kv in range(2):
            for j in range(4):
                part = (kb, vb)[kv].at[z, j, pl.ds(core * TOK, TOK), :]
                remote(part, part, s1s.at[kv, 0], s1r.at[kv, j], c, h).wait_recv()
            for step in (0, 1):
                z_copy(kv, step).start()
        b_start(0)

    def w_copy(kv):
        return remote(
            (k_win, v_win)[kv], (wk, wv)[kv].at[0], ws.at[kv, 0], wr.at[kv, 0], c + 2, h
        )

    def w_start():
        for kv in range(2):
            @pl.when(c + 2 < CTX)
            def _():
                w_copy(kv).start()

    def y_copy(kv, slot):
        ref = (wk, wv)[kv]
        return remote(ref.at[slot], ref.at[1], ws.at[kv, 1], wr.at[kv, 1], partner(0), h)

    def w_arrive():
        for kv in range(2):
            ref = (wk, wv)[kv]

            @pl.when(c >= 2)
            def _():
                w_copy(kv).wait_recv()

            @pl.when(c < 2)
            def _():
                ref[0] = jnp.zeros((TOK, GROUPS * D), bf16)

            @pl.when(yh == 1)
            def _():
                y_copy(kv, 0).start()

    w_start()
    q_start(0)
    own_chunk()
    for t in range(1, 4):
        q_start(t)
    fenwick(0)
    for i in (3, 4, 5):
        loads[i].wait()

    step_row = lax.broadcasted_iota(jnp.int32, (TOK, 2 * TOK), 0) + core * TOK
    step_col = lax.broadcasted_iota(jnp.int32, (TOK, 2 * TOK), 1)
    step_mask = step_col <= step_row

    def attend(blk, chunk, parts, first):
        size = parts * 2 * TOK
        kk = kb[chunk, :parts].reshape(size, D)
        vv = vb[chunk, :parts].reshape(size, D)
        vv = jnp.concatenate([vv, jnp.ones((size, D), bf16)], axis=1)

        def scores(r):
            return dot(qb[blk, :, r * D : (r + 1) * D], kk, 1, 1)

        nxt = scores(0)
        for r in range(PER):
            s = nxt
            if r + 1 < PER:
                nxt = scores(r + 1)
            sl = pl.ds(r * TOK, TOK)
            if first:
                last = jnp.where(step_mask, s[:, size - 2 * TOK :], NEG)
                s = last if parts == 1 else jnp.concatenate([s[:, : size - 2 * TOK], last], axis=1)
                new = jnp.max(s, axis=1, keepdims=True)
            else:
                old = mx[blk, sl, :][:, :1]
                new = jnp.maximum(old, jnp.max(s, axis=1, keepdims=True))
            p = jnp.exp2(s * EXP2_SCALE - new * EXP2_SCALE).astype(bf16)
            o = dot(p, vv, 1, 0)
            if not first:
                o += acc[blk, sl, :] * jnp.exp2((old - new) * EXP2_SCALE)
            acc[blk, sl, :] = o
            mx[blk, sl, :] = jnp.broadcast_to(new, (TOK, D))

    def r_copy(blk):
        return remote(
            ob.at[blk], cr.at[x], rs.at[blk], rr.at[x],
            blk * 8 + z * 2 + core, role_head,
        )

    def send_back(blk):
        for r in range(PER):
            sl = pl.ds(r * TOK, TOK)
            ob[blk, :, r * D : (r + 1) * D] = (acc[blk, sl, :D] / acc[blk, sl, D:]).astype(bf16)
        local = mixed & (x == blk)

        @pl.when(local)
        def _():
            pltpu.make_async_copy(ob.at[blk], cr.at[x], rr.at[x]).start()

        @pl.when(jnp.logical_not(local))
        def _():
            r_copy(blk).start()

    def w_y_start():
        for kv in range(2):
            @pl.when(yh == 0)
            def _():
                y_copy(kv, 2).start()

    events = {
        0: [lambda: b_wait(0)],
        1: [lambda: fenwick(1)],
        2: [w_y_start],
        3: [lambda: fenwick(2), w_arrive],
        4: [lambda: b_start(1), lambda: b_start(2), lambda: b_wait(1)],
        6: [lambda: fenwick(3)],
        8: [lambda: b_wait(2)],
        10: [lambda: fenwick(4), lambda: b_start(3)],
        12: [lambda: b_wait(3)],
    }

    def step(i, carry):
        n = i // 4
        chunk = z_of(n)
        blk = (x + i + jnp.where(n == 3, 1, 0)) % 4
        for at, todo in events.items():
            @pl.when(i == at)
            def _():
                for do in todo:
                    do()

        @pl.when(n == 0)
        def _():
            remote(
                q_cross.at[:, pl.ds(0, GC)], qb.at[blk], qs.at[0], qr.at[blk], c, h
            ).wait_recv()
            for j in range(4):
                @pl.when(blk == j)
                def _():
                    attend(blk, chunk, j + 1, True)

        @pl.when(n > 0)
        def _():
            parts = blk + jnp.where(chunk < z, 1, 0)
            for j in range(1, 5):
                @pl.when(parts == j)
                def _():
                    attend(blk, chunk, j, False)

        @pl.when(n == 3)
        def _():
            send_back(blk)

        return carry

    lax.fori_loop(0, 16, step, 0)

    for level in range(5):
        scale = jnp.where((c // 2**level) % 2 == 1, (D * TOK * 2**level) ** -0.5, 0.0)
        for g in range(GROUPS):
            bucket = fr[level, g]
            for r in range(PER):
                hd = g * PER + r
                term = dot(ql[:, hd * D : (hd + 1) * D], bucket, 1, 0)
                at = hd * LEVELS + level + 1
                comb[:, hd * D : (hd + 1) * D] += (lw[:, at : at + 1] * scale) * term

    for kv in range(2):
        y_copy(kv, 0).wait_recv()

    far = 3 * TOK
    row = lax.broadcasted_iota(jnp.int32, (TOK, far), 0) + 2 * TOK
    col = lax.broadcasted_iota(jnp.int32, (TOK, far), 1)
    band = (col <= row) & (col > row - W) & (col >= (2 - c) * TOK)
    ones = jnp.ones((far, D), bf16)

    def window_group(g):
        kk = wk[:, :, g * D : (g + 1) * D].reshape(far, D)
        vv = jnp.concatenate([wv[:, :, g * D : (g + 1) * D].reshape(far, D), ones], axis=1)

        def scores(r):
            hd = g * PER + r
            return dot(qw[:, hd * D : (hd + 1) * D], kk, 1, 1)

        nxt = scores(0)
        for r in range(PER):
            s = nxt
            if r + 1 < PER:
                nxt = scores(r + 1)
            hd = g * PER + r
            s = jnp.where(band, s, NEG)
            top = jnp.max(s, axis=1, keepdims=True)
            p = jnp.exp2(s * EXP2_SCALE - top * EXP2_SCALE).astype(bf16)
            o = dot(p, vv, 1, 0)
            comb[:, hd * D : (hd + 1) * D] += o[:, :D] / o[:, D:]

    for g in range(GROUPS):
        window_group(g)


    square = jnp.zeros((TOK, D), f32)
    for j in range(4):
        remote(ob.at[j], cr.at[j], rs.at[j], rr.at[j], c, h).wait_recv()
        for r in range(PER):
            hd = j * PER + r
            at = slice(hd * D, (hd + 1) * D)
            v = (comb[:, at] + cr[j, :, r * D : (r + 1) * D].astype(f32)) * gain[hd]
            comb[:, at] = v
            square += v * v
    hs[...] = dot(jnp.ones((8, D), f32), square, 1, 1, lax.Precision.HIGHEST)
    for d in range(1, 4):
        remote(hs, hr.at[d - 1], hss.at[d - 1], hrs.at[d - 1], c, (h + d) % 4).start()
    total = hs[...]
    for d in range(1, 4):
        remote(hs, hr.at[d - 1], hss.at[d - 1], hrs.at[d - 1], c, (h + d) % 4).wait_recv()
        total = total + hr[d - 1]
    norm = lax.rsqrt(total / (4 * HEADS * D) + 1e-6).T[:, :1]
    for hd in range(HEADS):
        at = slice(hd * D, (hd + 1) * D)
        out[:, at] = (comb[:, at] * norm).astype(bf16)

    for j in range(4):
        local = mixed & (x == j)

        @pl.when(jnp.logical_not(local))
        def _():
            for kv in range(2):
                src, dst = s1_copy(j, kv)
                remote(src, dst, s1s.at[kv, j], s1r.at[kv, x], c, h).wait_send()
            r_copy(j).wait_send()
        for kv in range(2):
            b_copy(kv, j).wait_send()
    for kv in range(2):
        for n in range(3):
            z_copy(kv, n).wait_send()

    @pl.when(jnp.logical_not(mixed))
    def _():
        remote(*q_copy(0)).wait_send()

    for t in range(1, 4):
        remote(*q_copy(t)).wait_send()
    for kv in range(2):
        y_copy(kv, 0).wait_send()

        @pl.when(c + 2 < CTX)
        def _():
            w_copy(kv).wait_send()
    for level in range(5):
        f_copy(level).wait_send()
    for d in range(1, 4):
        remote(hs, hr.at[d - 1], hss.at[d - 1], hrs.at[d - 1], c, h).wait_send()


def per_device(
    q_win, k_win, v_win, q_lin, k_lin, v_lin, level_table, level_index, q_cross, k_shared,
    v_shared, head_gain,
):
    dma = pltpu.SemaphoreType.DMA
    whole = pl.BlockSpec(memory_space=pl.ANY)
    vmem = pl.BlockSpec(memory_space=pltpu.VMEM)
    smem = pl.BlockSpec(memory_space=pltpu.SMEM)
    kv = GROUPS * D
    return pl.pallas_call(
        kernel,
        out_shape=jax.ShapeDtypeStruct((TOK, HEADS * D), bf16),
        in_specs=[whole] * 6 + [vmem, vmem] + [whole] * 3 + [smem],
        out_specs=vmem,
        scratch_shapes=[
            pltpu.VMEM((TOK, HEADS * D), bf16),
            pltpu.VMEM((TOK, kv), bf16),
            pltpu.VMEM((TOK, kv), bf16),
            pltpu.VMEM((TOK, HEADS * D), bf16),
            pltpu.VMEM((3, TOK, kv), bf16),
            pltpu.VMEM((3, TOK, kv), bf16),
            pltpu.VMEM((4, TOK, GC), bf16),
            pltpu.VMEM((4, 4, 2 * TOK, D), bf16),
            pltpu.VMEM((4, 4, 2 * TOK, D), bf16),
            pltpu.VMEM((4, TOK, GC), bf16),
            pltpu.VMEM((4, TOK, GC), bf16),
            pltpu.VMEM((4, PER * TOK, 2 * D), f32),
            pltpu.VMEM((4, PER * TOK, D), f32),
            pltpu.VMEM((TOK, HEADS * D), f32),
            pltpu.VMEM((TOK, HEADS * LEVELS), f32),
            pltpu.VMEM((GROUPS, D, D), f32),
            pltpu.VMEM((5, GROUPS, D, D), bf16),
            pltpu.VMEM((5, GROUPS, D, D), bf16),
            pltpu.VMEM((8, TOK), f32),
            pltpu.VMEM((3, 8, TOK), f32),
            dma((6,)),
            dma((2, 4)), dma((2, 4)),
            dma((2, 2)), dma((2, 2)),
            dma((4,)), dma((4,)),
            dma((5,)), dma((5,)),
            dma((2, 3)), dma((2, 3)),
            dma((2, 4)), dma((2, 4)),
            dma((4,)), dma((4,)),
            dma((3,)), dma((3,)),
        ],
        compiler_params=pltpu.CompilerParams(
            collective_id=0, has_side_effects=True, vmem_limit_bytes=56 * 2**20
        ),
        name="hybrid_attention",
    )(
        q_win, k_win, v_win, q_lin, k_lin, v_lin,
        level_table.reshape(level_table.shape[0], -1), level_index.reshape(1, -1),
        q_cross, k_shared, v_shared, head_gain,
    )


def solution(mesh):
    return jax.shard_map(
        per_device,
        mesh=mesh,
        in_specs=(
            P("ctx", "head"),
            P("ctx", "head"),
            P("ctx", "head"),
            P("ctx", "head"),
            P("ctx", "head"),
            P("ctx", "head"),
            P(None, "head", None),
            P("ctx"),
            P("ctx", "head"),
            P("ctx", "head"),
            P("ctx", "head"),
            P("head"),
        ),
        out_specs=P("ctx", "head"),
        check_vma=False,
    )
```

```python
import jax
import jax.numpy as jnp
from jax import lax
from jax.experimental import pallas as pl
from jax.experimental.pallas import tpu as pltpu
from jax.sharding import PartitionSpec as P

bf16 = jnp.bfloat16
f32 = jnp.float32
TOK = 256
D = 128
HEADS = 16
GROUPS = 4
PER = 4
GC = PER * D
LEVELS = 6
W = 512
CTX = 32
NEG = -1e30
EXP2_SCALE = D**-0.5 * 1.4426950408889634


def dot(a, b, ca, cb, precision=None):
    return lax.dot_general(
        a, b, (((ca,), (cb,)), ((), ())), preferred_element_type=f32, precision=precision
    )


def kernel(
    q_win, k_win, v_win, q_lin, k_lin, v_lin, table, index, q_cross, k_sh, v_sh, gain,
    comb, norm,
    ql, kl, vl, qw, wk, wv, qb, kb, vb, ob, cr, acc, mx, lw,
    state, fs, fr, hs, hr,
    in_sem, s1s, s1r, ws, wr, qs, qr, fss, frs, zs, zr, fs2, fr2, bs, br, rs, rr, hss, hrs,
):
    c = lax.axis_index("ctx")
    h = lax.axis_index("head")
    x, z, yh = c // 8, (c // 2) % 4, c % 2
    ylo, core = h // 2, h % 2
    role_head = ylo * 2 + yh
    mixed = core == yh

    def remote(src, dst, ssem, rsem, cc, hh):
        return pltpu.make_async_remote_copy(
            src_ref=src, dst_ref=dst, send_sem=ssem, recv_sem=rsem,
            device_id=(cc, hh), device_id_type=pl.DeviceIdType.MESH,
        )

    loads = [
        (k_lin, kl), (v_lin, vl), (q_lin, ql), (k_win, wk.at[2]), (v_win, wv.at[2]), (q_win, qw),
    ]
    loads = [pltpu.make_async_copy(s, d, in_sem.at[i]) for i, (s, d) in enumerate(loads)]
    for copy in loads:
        copy.start()

    barrier = pltpu.get_barrier_semaphore()

    def greet(cc, hh):
        pl.semaphore_signal(
            barrier, inc=1, device_id=(cc, hh), device_id_type=pl.DeviceIdType.MESH
        )

    def partner(level):
        bit = 2**level
        return c + bit - 2 * bit * ((c // bit) % 2)

    for j in range(4):
        @pl.when(jnp.logical_not(mixed & (x == j)))
        def _():
            greet(j * 8 + z * 2 + core, role_head)

    @pl.when(jnp.logical_not(mixed))
    def _():
        greet(partner(3), h)
        greet(partner(4), h)

    for dz in range(1, 4):
        greet(x * 8 + (z + dz) % 4 * 2 + yh, h)
        greet(c, (h + dz) % 4)
    greet(partner(0), h)

    @pl.when(z == 3)
    def _():
        greet((c + 2) % CTX, h)

    @pl.when(z == 0)
    def _():
        greet((c + CTX - 2) % CTX, h)

    loads[0].wait()
    loads[1].wait()
    for g in range(GROUPS):
        own = dot(kl[:, g * D : (g + 1) * D], vl[:, g * D : (g + 1) * D], 0, 0)
        state[g] = own
        fs[0, g] = own.astype(bf16)

    pl.semaphore_wait(
        barrier,
        jnp.where(mixed, 3, 6) + 7 + jnp.where((z == 0) | (z == 3), 1, 0),
    )

    def s1_copy(j, kv):
        src = (k_sh, v_sh)[kv].at[:, pl.ds(j * D, D)]
        dst = (kb, vb)[kv].at[z, x, pl.ds(yh * TOK, TOK), :]
        return src, dst

    def f_copy(level):
        return remote(
            fs.at[level], fr.at[level], fss.at[level], frs.at[level], partner(level), h
        )

    def fenwick(level):
        f_copy(level).wait_recv()
        got = fr[level]
        if level < 4:
            total = state[...] + got.astype(f32)
            state[...] = total
            fs[level + 1] = total.astype(bf16)
            f_copy(level + 1).start()

    for j in range(4):
        for kv in range(2):
            src, dst = s1_copy(j, kv)
            local = mixed & (x == j)

            @pl.when(local)
            def _():
                pltpu.make_async_copy(src, dst, s1r.at[kv, j]).start()

            @pl.when(jnp.logical_not(local))
            def _():
                remote(
                    src, dst, s1s.at[kv, j], s1r.at[kv, x], j * 8 + z * 2 + core, role_head
                ).start()

    def q_copy(t):
        j = (x + 4 - t) % 4
        return (
            q_cross.at[:, pl.ds(j * GC, GC)], qb.at[x], qs.at[t], qr.at[x],
            j * 8 + z * 2 + core, role_head,
        )

    def q_start(t):
        src, dst, ssem, rsem, cc, hh = q_copy(t)
        if t == 0:
            @pl.when(mixed)
            def _():
                pltpu.make_async_copy(src, dst, rsem).start()

            @pl.when(jnp.logical_not(mixed))
            def _():
                remote(src, dst, ssem, rsem, cc, hh).start()
        else:
            remote(src, dst, ssem, rsem, cc, hh).start()

    def z_copy(kv, step, j):
        part = (kb, vb)[kv].at[z, j, pl.ds(core * TOK, TOK), :]
        return remote(
            part, part, zs.at[kv, step, j], zr.at[kv, step, j],
            x * 8 + (z + 1 + 2 * step) % 4 * 2 + yh, h,
        )

    def z_forward(kv):
        tile, to = ((z + 1) % 4, (z + 3) % 4) if kv == 0 else ((z + 3) % 4, (z + 1) % 4)
        part = (kb, vb)[kv].at[tile, :, pl.ds(core * TOK, TOK), :]
        return remote(part, part, fs2.at[kv], fr2.at[kv], x * 8 + to * 2 + yh, h)

    def z_of(n):
        return (z + jnp.where(n == 1, 3, jnp.where(n == 2, 1, jnp.where(n == 3, 2, 0)))) % 4

    def b_copy(kv, n):
        part = (kb, vb)[kv].at[z_of(n), :, pl.ds(core * TOK, TOK), :]
        return remote(part, part, bs.at[kv, n], br.at[kv, n], c, h + 1 - 2 * core)

    def b_start(n):
        for kv in range(2):
            if n == 3:
                z_forward(kv).wait_recv()
            elif n > 0:
                for j in range(4):
                    z_copy(kv, n - 1, j).wait_recv()
            b_copy(kv, n).start()
        if n == 1:
            z_forward(1).start()
        if n == 2:
            z_forward(0).start()

    def b_wait(n):
        for kv in range(2):
            b_copy(kv, n).wait_recv()

    def own_chunk():
        for d in (0, 1, 3, 2):
            j = (x + d) % 4
            for kv in range(2):
                part = (kb, vb)[kv].at[z, j, pl.ds(core * TOK, TOK), :]
                remote(part, part, s1s.at[kv, 0], s1r.at[kv, j], c, h).wait_recv()
                for step in (0, 1):
                    z_copy(kv, step, j).start()
        b_start(0)

    def w_copy(kv):
        return remote(
            (k_win, v_win)[kv], (wk, wv)[kv].at[0], ws.at[kv, 0], wr.at[kv, 0], c + 2, h
        )

    def w_start():
        for kv in range(2):
            @pl.when(c + 2 < CTX)
            def _():
                w_copy(kv).start()

    def y_copy(kv, slot):
        ref = (wk, wv)[kv]
        return remote(ref.at[slot], ref.at[1], ws.at[kv, 1], wr.at[kv, 1], partner(0), h)

    def w_arrive():
        for kv in range(2):
            ref = (wk, wv)[kv]

            @pl.when(c >= 2)
            def _():
                w_copy(kv).wait_recv()

            @pl.when(c < 2)
            def _():
                ref[0] = jnp.zeros((TOK, GROUPS * D), bf16)

            @pl.when(yh == 1)
            def _():
                y_copy(kv, 0).start()

    w_start()

    hot = (lax.broadcasted_iota(jnp.int32, (64, TOK), 0) == index[...]).astype(f32)
    lw[...] = dot(hot, table[...], 0, 0, lax.Precision.HIGHEST)

    loads[2].wait()
    rows = lax.broadcasted_iota(jnp.int32, (TOK, TOK), 0)
    cols = lax.broadcasted_iota(jnp.int32, (TOK, TOK), 1)
    causal = rows >= cols
    for g in range(GROUPS):
        for r in range(PER):
            hd = g * PER + r
            s = dot(ql[:, hd * D : (hd + 1) * D], kl[:, g * D : (g + 1) * D], 1, 1)
            s = jnp.where(causal, s * (D * TOK) ** -0.5, 0.0).astype(bf16)
            comb[:, hd * D : (hd + 1) * D] = lw[:, hd * LEVELS : hd * LEVELS + 1] * dot(
                s, vl[:, g * D : (g + 1) * D], 1, 0
            )

    own_chunk()
    for t in range(4):
        q_start(t)
    f_copy(0).start()
    for i in (3, 4, 5):
        loads[i].wait()

    step_row = lax.broadcasted_iota(jnp.int32, (TOK, 2 * TOK), 0) + core * TOK
    step_col = lax.broadcasted_iota(jnp.int32, (TOK, 2 * TOK), 1)
    step_mask = step_col <= step_row

    def attend(blk, chunk, parts, first):
        size = parts * 2 * TOK
        kk = kb[chunk, :parts].reshape(size, D)
        vv = vb[chunk, :parts].reshape(size, D)
        vv = jnp.concatenate([vv, jnp.ones((size, D), bf16)], axis=1)

        def scores(r):
            return dot(qb[blk, :, r * D : (r + 1) * D], kk, 1, 1)

        nxt = scores(0)
        for r in range(PER):
            s = nxt
            if r + 1 < PER:
                nxt = scores(r + 1)
            sl = pl.ds(r * TOK, TOK)
            if first:
                last = jnp.where(step_mask, s[:, size - 2 * TOK :], NEG)
                s = last if parts == 1 else jnp.concatenate([s[:, : size - 2 * TOK], last], axis=1)
                new = jnp.max(s, axis=1, keepdims=True)
            else:
                old = mx[blk, sl, :][:, :1]
                new = jnp.maximum(old, jnp.max(s, axis=1, keepdims=True))
            p = jnp.exp2(s * EXP2_SCALE - new * EXP2_SCALE).astype(bf16)
            o = dot(p, vv, 1, 0)
            if not first:
                o += acc[blk, sl, :] * jnp.exp2((old - new) * EXP2_SCALE)
            acc[blk, sl, :] = o
            mx[blk, sl, :] = jnp.broadcast_to(new, (TOK, D))

    def r_copy(blk):
        return remote(
            ob.at[blk], cr.at[x], rs.at[blk], rr.at[x],
            blk * 8 + z * 2 + core, role_head,
        )

    def send_back(blk):
        for r in range(PER):
            sl = pl.ds(r * TOK, TOK)
            ob[blk, :, r * D : (r + 1) * D] = (acc[blk, sl, :D] / acc[blk, sl, D:]).astype(bf16)
        local = mixed & (x == blk)

        @pl.when(local)
        def _():
            pltpu.make_async_copy(ob.at[blk], cr.at[x], rr.at[x]).start()

        @pl.when(jnp.logical_not(local))
        def _():
            r_copy(blk).start()

    def w_y_start():
        for kv in range(2):
            @pl.when(yh == 0)
            def _():
                y_copy(kv, 2).start()

    events = {
        0: [lambda: b_wait(0)],
        2: [w_y_start],
        3: [lambda: fenwick(0), w_arrive],
        4: [lambda: b_start(1), lambda: b_start(2), lambda: b_wait(1)],
        5: [lambda: fenwick(1)],
        7: [lambda: fenwick(2)],
        8: [lambda: b_wait(2)],
        9: [lambda: fenwick(3)],
        11: [lambda: b_start(3)],
        12: [lambda: b_wait(3), lambda: fenwick(4)],
    }

    def step(i, carry):
        n = i // 4
        chunk = z_of(n)
        blk = (x + i + jnp.where(n == 3, 1, 0)) % 4
        for at, todo in events.items():
            @pl.when(i == at)
            def _():
                for do in todo:
                    do()

        @pl.when(n == 0)
        def _():
            remote(
                q_cross.at[:, pl.ds(0, GC)], qb.at[blk], qs.at[0], qr.at[blk], c, h
            ).wait_recv()
            for j in range(4):
                @pl.when(blk == j)
                def _():
                    attend(blk, chunk, j + 1, True)

        @pl.when(n > 0)
        def _():
            parts = blk + jnp.where(chunk < z, 1, 0)
            for j in range(1, 5):
                @pl.when(parts == j)
                def _():
                    attend(blk, chunk, j, False)

        @pl.when(n == 3)
        def _():
            send_back(blk)

        return carry

    lax.fori_loop(0, 16, step, 0)

    for level in range(5):
        scale = jnp.where((c // 2**level) % 2 == 1, (D * TOK * 2**level) ** -0.5, 0.0)
        for g in range(GROUPS):
            bucket = fr[level, g]
            for r in range(PER):
                hd = g * PER + r
                term = dot(ql[:, hd * D : (hd + 1) * D], bucket, 1, 0)
                at = hd * LEVELS + level + 1
                comb[:, hd * D : (hd + 1) * D] += (lw[:, at : at + 1] * scale) * term

    for kv in range(2):
        y_copy(kv, 0).wait_recv()

    far = 3 * TOK
    row = lax.broadcasted_iota(jnp.int32, (TOK, far), 0) + 2 * TOK
    col = lax.broadcasted_iota(jnp.int32, (TOK, far), 1)
    band = (col <= row) & (col > row - W) & (col >= (2 - c) * TOK)
    ones = jnp.ones((far, D), bf16)

    def window_group(g):
        kk = wk[:, :, g * D : (g + 1) * D].reshape(far, D)
        vv = jnp.concatenate([wv[:, :, g * D : (g + 1) * D].reshape(far, D), ones], axis=1)

        def scores(r):
            hd = g * PER + r
            return dot(qw[:, hd * D : (hd + 1) * D], kk, 1, 1)

        nxt = scores(0)
        for r in range(PER):
            s = nxt
            if r + 1 < PER:
                nxt = scores(r + 1)
            hd = g * PER + r
            s = jnp.where(band, s, NEG)
            top = jnp.max(s, axis=1, keepdims=True)
            p = jnp.exp2(s * EXP2_SCALE - top * EXP2_SCALE).astype(bf16)
            o = dot(p, vv, 1, 0)
            comb[:, hd * D : (hd + 1) * D] += o[:, :D] / o[:, D:]

    for g in range(GROUPS):
        window_group(g)


    square = jnp.zeros((TOK, D), f32)
    for j in range(4):
        remote(ob.at[j], cr.at[j], rs.at[j], rr.at[j], c, h).wait_recv()
        for r in range(PER):
            hd = j * PER + r
            at = slice(hd * D, (hd + 1) * D)
            v = (comb[:, at] + cr[j, :, r * D : (r + 1) * D].astype(f32)) * gain[hd]
            comb[:, at] = v
            square += v * v
    hs[...] = dot(jnp.ones((8, D), f32), square, 1, 1, lax.Precision.HIGHEST)
    for d in range(1, 4):
        remote(hs, hr.at[d - 1], hss.at[d - 1], hrs.at[d - 1], c, (h + d) % 4).start()
    total = hs[...]
    for d in range(1, 4):
        remote(hs, hr.at[d - 1], hss.at[d - 1], hrs.at[d - 1], c, (h + d) % 4).wait_recv()
        total = total + hr[d - 1]
    norm[...] = lax.rsqrt(total / (4 * HEADS * D) + 1e-6).T

    for j in range(4):
        local = mixed & (x == j)

        @pl.when(jnp.logical_not(local))
        def _():
            for kv in range(2):
                src, dst = s1_copy(j, kv)
                remote(src, dst, s1s.at[kv, j], s1r.at[kv, x], c, h).wait_send()
            r_copy(j).wait_send()
        for kv in range(2):
            b_copy(kv, j).wait_send()
    for kv in range(2):
        z_forward(kv).wait_send()
        for j in range(4):
            for n in range(2):
                z_copy(kv, n, j).wait_send()

    @pl.when(jnp.logical_not(mixed))
    def _():
        remote(*q_copy(0)).wait_send()

    for t in range(1, 4):
        remote(*q_copy(t)).wait_send()
    for kv in range(2):
        y_copy(kv, 0).wait_send()

        @pl.when(c + 2 < CTX)
        def _():
            w_copy(kv).wait_send()
    for level in range(5):
        f_copy(level).wait_send()
    for d in range(1, 4):
        remote(hs, hr.at[d - 1], hss.at[d - 1], hrs.at[d - 1], c, h).wait_send()


def per_device(
    q_win, k_win, v_win, q_lin, k_lin, v_lin, level_table, level_index, q_cross, k_shared,
    v_shared, head_gain,
):
    dma = pltpu.SemaphoreType.DMA
    whole = pl.BlockSpec(memory_space=pl.ANY)
    vmem = pl.BlockSpec(memory_space=pltpu.VMEM)
    smem = pl.BlockSpec(memory_space=pltpu.SMEM)
    kv = GROUPS * D
    comb, norm = pl.pallas_call(
        kernel,
        out_shape=[
            jax.ShapeDtypeStruct((TOK, HEADS * D), f32),
            jax.ShapeDtypeStruct((TOK, 8), f32),
        ],
        in_specs=[whole] * 6 + [vmem, vmem] + [whole] * 3 + [smem],
        out_specs=[vmem, vmem],
        scratch_shapes=[
            pltpu.VMEM((TOK, HEADS * D), bf16),
            pltpu.VMEM((TOK, kv), bf16),
            pltpu.VMEM((TOK, kv), bf16),
            pltpu.VMEM((TOK, HEADS * D), bf16),
            pltpu.VMEM((3, TOK, kv), bf16),
            pltpu.VMEM((3, TOK, kv), bf16),
            pltpu.VMEM((4, TOK, GC), bf16),
            pltpu.VMEM((4, 4, 2 * TOK, D), bf16),
            pltpu.VMEM((4, 4, 2 * TOK, D), bf16),
            pltpu.VMEM((4, TOK, GC), bf16),
            pltpu.VMEM((4, TOK, GC), bf16),
            pltpu.VMEM((4, PER * TOK, 2 * D), f32),
            pltpu.VMEM((4, PER * TOK, D), f32),
            pltpu.VMEM((TOK, HEADS * LEVELS), f32),
            pltpu.VMEM((GROUPS, D, D), f32),
            pltpu.VMEM((5, GROUPS, D, D), bf16),
            pltpu.VMEM((5, GROUPS, D, D), bf16),
            pltpu.VMEM((8, TOK), f32),
            pltpu.VMEM((3, 8, TOK), f32),
            dma((6,)),
            dma((2, 4)), dma((2, 4)),
            dma((2, 2)), dma((2, 2)),
            dma((4,)), dma((4,)),
            dma((5,)), dma((5,)),
            dma((2, 2, 4)), dma((2, 2, 4)),
            dma((2,)), dma((2,)),
            dma((2, 4)), dma((2, 4)),
            dma((4,)), dma((4,)),
            dma((3,)), dma((3,)),
        ],
        compiler_params=pltpu.CompilerParams(
            collective_id=0, has_side_effects=True, vmem_limit_bytes=56 * 2**20
        ),
        name="hybrid_attention",
    )(
        q_win, k_win, v_win, q_lin, k_lin, v_lin,
        level_table.reshape(level_table.shape[0], -1), level_index.reshape(1, -1),
        q_cross, k_shared, v_shared, head_gain,
    )
    return (comb * norm[:, :1]).astype(bf16)


def solution(mesh):
    return jax.shard_map(
        per_device,
        mesh=mesh,
        in_specs=(
            P("ctx", "head"),
            P("ctx", "head"),
            P("ctx", "head"),
            P("ctx", "head"),
            P("ctx", "head"),
            P("ctx", "head"),
            P(None, "head", None),
            P("ctx"),
            P("ctx", "head"),
            P("ctx", "head"),
            P("ctx", "head"),
            P("head"),
        ),
        out_specs=P("ctx", "head"),
        check_vma=False,
    )
```

```python
import jax
import jax.numpy as jnp
from jax import lax
from jax.experimental import pallas as pl
from jax.experimental.pallas import tpu as pltpu
from jax.sharding import PartitionSpec as P

bf16 = jnp.bfloat16
f32 = jnp.float32
TOK = 256
D = 128
HEADS = 16
GROUPS = 4
PER = 4
GC = PER * D
LEVELS = 6
W = 512
CTX = 32
NEG = -1e30
EXP2_SCALE = D**-0.5 * 1.4426950408889634


def dot(a, b, ca, cb, precision=None):
    return lax.dot_general(
        a, b, (((ca,), (cb,)), ((), ())), preferred_element_type=f32, precision=precision
    )


def kernel(
    q_win, k_win, v_win, q_lin, k_lin, v_lin, table, index, q_cross, k_sh, v_sh, gain,
    out,
    ql, kl, vl, qw, wk, wv, qb, kb, vb, ob, cr, acc, mx, comb, lw,
    state, fs, fr, hs, hr,
    in_sem, s1s, s1r, ws, wr, qs, qr, fss, frs, zs, zr, bs, br, rs, rr, hss, hrs,
):
    c = lax.axis_index("ctx")
    h = lax.axis_index("head")
    x, z, yh = c // 8, (c // 2) % 4, c % 2
    ylo, core = h // 2, h % 2
    role_head = ylo * 2 + yh
    mixed = core == yh

    def remote(src, dst, ssem, rsem, cc, hh):
        return pltpu.make_async_remote_copy(
            src_ref=src, dst_ref=dst, send_sem=ssem, recv_sem=rsem,
            device_id=(cc, hh), device_id_type=pl.DeviceIdType.MESH,
        )

    loads = [
        (k_lin, kl), (v_lin, vl), (q_lin, ql), (k_win, wk.at[2]), (v_win, wv.at[2]), (q_win, qw),
    ]
    loads = [pltpu.make_async_copy(s, d, in_sem.at[i]) for i, (s, d) in enumerate(loads)]
    for copy in loads:
        copy.start()

    barrier = pltpu.get_barrier_semaphore()

    def greet(cc, hh):
        pl.semaphore_signal(
            barrier, inc=1, device_id=(cc, hh), device_id_type=pl.DeviceIdType.MESH
        )

    def partner(level):
        bit = 2**level
        return c + bit - 2 * bit * ((c // bit) % 2)

    for j in range(4):
        @pl.when(jnp.logical_not(mixed & (x == j)))
        def _():
            greet(j * 8 + z * 2 + core, role_head)

    @pl.when(jnp.logical_not(mixed))
    def _():
        greet(partner(3), h)
        greet(partner(4), h)

    for dz in range(1, 4):
        greet(x * 8 + (z + dz) % 4 * 2 + yh, h)
        greet(c, (h + dz) % 4)
    greet(partner(0), h)

    @pl.when(z == 3)
    def _():
        greet((c + 2) % CTX, h)

    @pl.when(z == 0)
    def _():
        greet((c + CTX - 2) % CTX, h)

    loads[0].wait()
    loads[1].wait()
    for g in range(GROUPS):
        own = dot(kl[:, g * D : (g + 1) * D], vl[:, g * D : (g + 1) * D], 0, 0)
        state[g] = own
        fs[0, g] = own.astype(bf16)

    pl.semaphore_wait(
        barrier,
        jnp.where(mixed, 3, 6) + 7 + jnp.where((z == 0) | (z == 3), 1, 0),
    )

    def s1_copy(j, kv):
        src = (k_sh, v_sh)[kv].at[:, pl.ds(j * D, D)]
        dst = (kb, vb)[kv].at[z, x, pl.ds(yh * TOK, TOK), :]
        return src, dst

    def f_copy(level):
        return remote(
            fs.at[level], fr.at[level], fss.at[level], frs.at[level], partner(level), h
        )

    def fenwick(level):
        f_copy(level).wait_recv()
        got = fr[level]
        if level < 4:
            total = state[...] + got.astype(f32)
            state[...] = total
            fs[level + 1] = total.astype(bf16)
            f_copy(level + 1).start()

    f_copy(0).start()

    for j in range(4):
        for kv in range(2):
            src, dst = s1_copy(j, kv)
            local = mixed & (x == j)

            @pl.when(local)
            def _():
                pltpu.make_async_copy(src, dst, s1r.at[kv, j]).start()

            @pl.when(jnp.logical_not(local))
            def _():
                remote(
                    src, dst, s1s.at[kv, j], s1r.at[kv, x], j * 8 + z * 2 + core, role_head
                ).start()

    def q_copy(t):
        j = (x + 4 - t) % 4
        return (
            q_cross.at[:, pl.ds(j * GC, GC)], qb.at[x], qs.at[t], qr.at[x],
            j * 8 + z * 2 + core, role_head,
        )

    def q_start(t):
        src, dst, ssem, rsem, cc, hh = q_copy(t)
        if t == 0:
            @pl.when(mixed)
            def _():
                pltpu.make_async_copy(src, dst, rsem).start()

            @pl.when(jnp.logical_not(mixed))
            def _():
                remote(src, dst, ssem, rsem, cc, hh).start()
        else:
            remote(src, dst, ssem, rsem, cc, hh).start()

    def z_copy(kv, step):
        if step == 2:
            tile, to = ((z + 1) % 4, (z + 3) % 4) if kv == 0 else ((z + 3) % 4, (z + 1) % 4)
        else:
            tile, to = z, (z + 1 + 2 * step) % 4
        part = (kb, vb)[kv].at[tile, :, pl.ds(core * TOK, TOK), :]
        return remote(
            part, part, zs.at[kv, step], zr.at[kv, step], x * 8 + to * 2 + yh, h
        )

    def z_of(n):
        return (z + jnp.where(n == 1, 1, jnp.where(n == 2, 3, jnp.where(n == 3, 2, 0)))) % 4

    def b_copy(kv, n):
        part = (kb, vb)[kv].at[z_of(n), :, pl.ds(core * TOK, TOK), :]
        return remote(part, part, bs.at[kv, n], br.at[kv, n], c, h + 1 - 2 * core)

    def b_start(n):
        for kv in range(2):
            if n > 0:
                z_copy(kv, (1, 0, 2)[n - 1]).wait_recv()
            b_copy(kv, n).start()
        if n in (1, 2):
            z_copy(n - 1, 2).start()

    def b_wait(n):
        for kv in range(2):
            b_copy(kv, n).wait_recv()

    def own_chunk():
        for kv in range(2):
            for j in range(4):
                part = (kb, vb)[kv].at[z, j, pl.ds(core * TOK, TOK), :]
                remote(part, part, s1s.at[kv, 0], s1r.at[kv, j], c, h).wait_recv()
            for step in (0, 1):
                z_copy(kv, step).start()
        b_start(0)

    def w_copy(kv):
        return remote(
            (k_win, v_win)[kv], (wk, wv)[kv].at[0], ws.at[kv, 0], wr.at[kv, 0], c + 2, h
        )

    def w_start():
        for kv in range(2):
            @pl.when(c + 2 < CTX)
            def _():
                w_copy(kv).start()

    def y_copy(kv, slot):
        ref = (wk, wv)[kv]
        return remote(ref.at[slot], ref.at[1], ws.at[kv, 1], wr.at[kv, 1], partner(0), h)

    def w_arrive():
        for kv in range(2):
            ref = (wk, wv)[kv]

            @pl.when(c >= 2)
            def _():
                w_copy(kv).wait_recv()

            @pl.when(c < 2)
            def _():
                ref[0] = jnp.zeros((TOK, GROUPS * D), bf16)

            @pl.when(yh == 1)
            def _():
                y_copy(kv, 0).start()

    w_start()
    q_start(0)

    hot = (lax.broadcasted_iota(jnp.int32, (64, TOK), 0) == index[...]).astype(f32)
    lw[...] = dot(hot, table[...], 0, 0, lax.Precision.HIGHEST)

    loads[2].wait()
    rows = lax.broadcasted_iota(jnp.int32, (TOK, TOK), 0)
    cols = lax.broadcasted_iota(jnp.int32, (TOK, TOK), 1)
    causal = rows >= cols
    for g in range(GROUPS):
        for r in range(PER):
            hd = g * PER + r
            s = dot(ql[:, hd * D : (hd + 1) * D], kl[:, g * D : (g + 1) * D], 1, 1)
            s = jnp.where(causal, s * (D * TOK) ** -0.5, 0.0).astype(bf16)
            comb[:, hd * D : (hd + 1) * D] = lw[:, hd * LEVELS : hd * LEVELS + 1] * dot(
                s, vl[:, g * D : (g + 1) * D], 1, 0
            )

    fenwick(0)
    fenwick(1)
    own_chunk()
    for t in range(1, 4):
        q_start(t)
    for i in (3, 4, 5):
        loads[i].wait()

    step_row = lax.broadcasted_iota(jnp.int32, (TOK, 2 * TOK), 0) + core * TOK
    step_col = lax.broadcasted_iota(jnp.int32, (TOK, 2 * TOK), 1)
    step_mask = step_col <= step_row

    def attend(blk, chunk, parts, first):
        size = parts * 2 * TOK
        kk = kb[chunk, :parts].reshape(size, D)
        vv = vb[chunk, :parts].reshape(size, D)
        vv = jnp.concatenate([vv, jnp.ones((size, D), bf16)], axis=1)

        def scores(r):
            return dot(qb[blk, :, r * D : (r + 1) * D], kk, 1, 1)

        nxt = scores(0)
        for r in range(PER):
            s = nxt
            if r + 1 < PER:
                nxt = scores(r + 1)
            sl = pl.ds(r * TOK, TOK)
            if first:
                last = jnp.where(step_mask, s[:, size - 2 * TOK :], NEG)
                s = last if parts == 1 else jnp.concatenate([s[:, : size - 2 * TOK], last], axis=1)
                new = jnp.max(s, axis=1, keepdims=True)
            else:
                old = mx[blk, sl, :][:, :1]
                new = jnp.maximum(old, jnp.max(s, axis=1, keepdims=True))
            p = jnp.exp2(s * EXP2_SCALE - new * EXP2_SCALE).astype(bf16)
            o = dot(p, vv, 1, 0)
            if not first:
                o += acc[blk, sl, :] * jnp.exp2((old - new) * EXP2_SCALE)
            acc[blk, sl, :] = o
            mx[blk, sl, :] = jnp.broadcast_to(new, (TOK, D))

    def r_copy(blk):
        return remote(
            ob.at[blk], cr.at[x], rs.at[blk], rr.at[x],
            blk * 8 + z * 2 + core, role_head,
        )

    def send_back(blk):
        for r in range(PER):
            sl = pl.ds(r * TOK, TOK)
            ob[blk, :, r * D : (r + 1) * D] = (acc[blk, sl, :D] / acc[blk, sl, D:]).astype(bf16)
        local = mixed & (x == blk)

        @pl.when(local)
        def _():
            pltpu.make_async_copy(ob.at[blk], cr.at[x], rr.at[x]).start()

        @pl.when(jnp.logical_not(local))
        def _():
            r_copy(blk).start()

    def w_y_start():
        for kv in range(2):
            @pl.when(yh == 0)
            def _():
                y_copy(kv, 2).start()

    events = {
        0: [lambda: b_wait(0)],
        1: [lambda: fenwick(2)],
        2: [w_y_start],
        3: [w_arrive],
        4: [lambda: b_start(1), lambda: b_wait(1)],
        5: [lambda: fenwick(3)],
        6: [lambda: b_start(2)],
        8: [lambda: b_wait(2)],
        9: [lambda: fenwick(4)],
        10: [lambda: b_start(3)],
        12: [lambda: b_wait(3)],
    }

    def step(i, carry):
        n = i // 4
        chunk = z_of(n)
        blk = (x + i + jnp.where(n == 3, 1, 0)) % 4
        for at, todo in events.items():
            @pl.when(i == at)
            def _():
                for do in todo:
                    do()

        @pl.when(n == 0)
        def _():
            remote(
                q_cross.at[:, pl.ds(0, GC)], qb.at[blk], qs.at[0], qr.at[blk], c, h
            ).wait_recv()
            for j in range(4):
                @pl.when(blk == j)
                def _():
                    attend(blk, chunk, j + 1, True)

        @pl.when(n > 0)
        def _():
            parts = blk + jnp.where(chunk < z, 1, 0)
            for j in range(1, 5):
                @pl.when(parts == j)
                def _():
                    attend(blk, chunk, j, False)

        @pl.when(n == 3)
        def _():
            send_back(blk)

        return carry

    lax.fori_loop(0, 16, step, 0)

    for level in range(5):
        scale = jnp.where((c // 2**level) % 2 == 1, (D * TOK * 2**level) ** -0.5, 0.0)
        for g in range(GROUPS):
            bucket = fr[level, g]
            for r in range(PER):
                hd = g * PER + r
                term = dot(ql[:, hd * D : (hd + 1) * D], bucket, 1, 0)
                at = hd * LEVELS + level + 1
                comb[:, hd * D : (hd + 1) * D] += (lw[:, at : at + 1] * scale) * term

    for kv in range(2):
        y_copy(kv, 0).wait_recv()

    far = 3 * TOK
    row = lax.broadcasted_iota(jnp.int32, (TOK, far), 0) + 2 * TOK
    col = lax.broadcasted_iota(jnp.int32, (TOK, far), 1)
    band = (col <= row) & (col > row - W) & (col >= (2 - c) * TOK)
    ones = jnp.ones((far, D), bf16)

    def window_group(g):
        kk = wk[:, :, g * D : (g + 1) * D].reshape(far, D)
        vv = jnp.concatenate([wv[:, :, g * D : (g + 1) * D].reshape(far, D), ones], axis=1)

        def scores(r):
            hd = g * PER + r
            return dot(qw[:, hd * D : (hd + 1) * D], kk, 1, 1)

        nxt = scores(0)
        for r in range(PER):
            s = nxt
            if r + 1 < PER:
                nxt = scores(r + 1)
            hd = g * PER + r
            s = jnp.where(band, s, NEG)
            top = jnp.max(s, axis=1, keepdims=True)
            p = jnp.exp2(s * EXP2_SCALE - top * EXP2_SCALE).astype(bf16)
            o = dot(p, vv, 1, 0)
            comb[:, hd * D : (hd + 1) * D] += o[:, :D] / o[:, D:]

    for g in range(GROUPS):
        window_group(g)


    square = jnp.zeros((TOK, D), f32)
    for j in range(4):
        remote(ob.at[j], cr.at[j], rs.at[j], rr.at[j], c, h).wait_recv()
        for r in range(PER):
            hd = j * PER + r
            at = slice(hd * D, (hd + 1) * D)
            v = (comb[:, at] + cr[j, :, r * D : (r + 1) * D].astype(f32)) * gain[hd]
            comb[:, at] = v
            square += v * v
    hs[...] = dot(jnp.ones((8, D), f32), square, 1, 1, lax.Precision.HIGHEST)
    for d in range(1, 4):
        remote(hs, hr.at[d - 1], hss.at[d - 1], hrs.at[d - 1], c, (h + d) % 4).start()
    total = hs[...]
    for d in range(1, 4):
        remote(hs, hr.at[d - 1], hss.at[d - 1], hrs.at[d - 1], c, (h + d) % 4).wait_recv()
        total = total + hr[d - 1]
    norm = lax.rsqrt(total / (4 * HEADS * D) + 1e-6).T[:, :1]
    for hd in range(HEADS):
        at = slice(hd * D, (hd + 1) * D)
        out[:, at] = (comb[:, at] * norm).astype(bf16)

    for j in range(4):
        local = mixed & (x == j)

        @pl.when(jnp.logical_not(local))
        def _():
            for kv in range(2):
                src, dst = s1_copy(j, kv)
                remote(src, dst, s1s.at[kv, j], s1r.at[kv, x], c, h).wait_send()
            r_copy(j).wait_send()
        for kv in range(2):
            b_copy(kv, j).wait_send()
    for kv in range(2):
        for n in range(3):
            z_copy(kv, n).wait_send()

    @pl.when(jnp.logical_not(mixed))
    def _():
        remote(*q_copy(0)).wait_send()

    for t in range(1, 4):
        remote(*q_copy(t)).wait_send()
    for kv in range(2):
        y_copy(kv, 0).wait_send()

        @pl.when(c + 2 < CTX)
        def _():
            w_copy(kv).wait_send()
    for level in range(5):
        f_copy(level).wait_send()
    for d in range(1, 4):
        remote(hs, hr.at[d - 1], hss.at[d - 1], hrs.at[d - 1], c, h).wait_send()


def per_device(
    q_win, k_win, v_win, q_lin, k_lin, v_lin, level_table, level_index, q_cross, k_shared,
    v_shared, head_gain,
):
    dma = pltpu.SemaphoreType.DMA
    whole = pl.BlockSpec(memory_space=pl.ANY)
    vmem = pl.BlockSpec(memory_space=pltpu.VMEM)
    smem = pl.BlockSpec(memory_space=pltpu.SMEM)
    kv = GROUPS * D
    return pl.pallas_call(
        kernel,
        out_shape=jax.ShapeDtypeStruct((TOK, HEADS * D), bf16),
        in_specs=[whole] * 6 + [vmem, vmem] + [whole] * 3 + [smem],
        out_specs=vmem,
        scratch_shapes=[
            pltpu.VMEM((TOK, HEADS * D), bf16),
            pltpu.VMEM((TOK, kv), bf16),
            pltpu.VMEM((TOK, kv), bf16),
            pltpu.VMEM((TOK, HEADS * D), bf16),
            pltpu.VMEM((3, TOK, kv), bf16),
            pltpu.VMEM((3, TOK, kv), bf16),
            pltpu.VMEM((4, TOK, GC), bf16),
            pltpu.VMEM((4, 4, 2 * TOK, D), bf16),
            pltpu.VMEM((4, 4, 2 * TOK, D), bf16),
            pltpu.VMEM((4, TOK, GC), bf16),
            pltpu.VMEM((4, TOK, GC), bf16),
            pltpu.VMEM((4, PER * TOK, 2 * D), f32),
            pltpu.VMEM((4, PER * TOK, D), f32),
            pltpu.VMEM((TOK, HEADS * D), f32),
            pltpu.VMEM((TOK, HEADS * LEVELS), f32),
            pltpu.VMEM((GROUPS, D, D), f32),
            pltpu.VMEM((5, GROUPS, D, D), bf16),
            pltpu.VMEM((5, GROUPS, D, D), bf16),
            pltpu.VMEM((8, TOK), f32),
            pltpu.VMEM((3, 8, TOK), f32),
            dma((6,)),
            dma((2, 4)), dma((2, 4)),
            dma((2, 2)), dma((2, 2)),
            dma((4,)), dma((4,)),
            dma((5,)), dma((5,)),
            dma((2, 3)), dma((2, 3)),
            dma((2, 4)), dma((2, 4)),
            dma((4,)), dma((4,)),
            dma((3,)), dma((3,)),
        ],
        compiler_params=pltpu.CompilerParams(
            collective_id=0, has_side_effects=True, vmem_limit_bytes=56 * 2**20
        ),
        name="hybrid_attention",
    )(
        q_win, k_win, v_win, q_lin, k_lin, v_lin,
        level_table.reshape(level_table.shape[0], -1), level_index.reshape(1, -1),
        q_cross, k_shared, v_shared, head_gain,
    )


def solution(mesh):
    return jax.shard_map(
        per_device,
        mesh=mesh,
        in_specs=(
            P("ctx", "head"),
            P("ctx", "head"),
            P("ctx", "head"),
            P("ctx", "head"),
            P("ctx", "head"),
            P("ctx", "head"),
            P(None, "head", None),
            P("ctx"),
            P("ctx", "head"),
            P("ctx", "head"),
            P("ctx", "head"),
            P("head"),
        ),
        out_specs=P("ctx", "head"),
        check_vma=False,
    )
```

```python
import jax
import jax.numpy as jnp
from jax import lax
from jax.experimental import pallas as pl
from jax.experimental.pallas import tpu as pltpu
from jax.sharding import PartitionSpec as P

bf16 = jnp.bfloat16
f32 = jnp.float32
TOK = 256
D = 128
HEADS = 16
GROUPS = 4
PER = 4
GC = PER * D
LEVELS = 6
W = 512
CTX = 32
NEG = -1e30
EXP2_SCALE = D**-0.5 * 1.4426950408889634


def dot(a, b, ca, cb, precision=None):
    return lax.dot_general(
        a, b, (((ca,), (cb,)), ((), ())), preferred_element_type=f32, precision=precision
    )


def kernel(
    q_win, k_win, v_win, q_lin, k_lin, v_lin, table, index, q_cross, k_sh, v_sh, gain,
    out,
    ql, kl, vl, qw, wk, wv, qb, kb, vb, ob, cr, acc, mx, comb, lw,
    state, fs, fr, hs, hr,
    in_sem, s1s, s1r, ws, wr, qs, qr, fss, frs, zs, zr, bs, br, rs, rr, hss, hrs,
):
    c = lax.axis_index("ctx")
    h = lax.axis_index("head")
    x, z, yh = c // 8, (c // 2) % 4, c % 2
    ylo, core = h // 2, h % 2
    role_head = ylo * 2 + yh
    mixed = core == yh

    def remote(src, dst, ssem, rsem, cc, hh):
        return pltpu.make_async_remote_copy(
            src_ref=src, dst_ref=dst, send_sem=ssem, recv_sem=rsem,
            device_id=(cc, hh), device_id_type=pl.DeviceIdType.MESH,
        )

    loads = [
        (k_lin, kl), (v_lin, vl), (q_lin, ql), (k_win, wk.at[2]), (v_win, wv.at[2]), (q_win, qw),
    ]
    loads = [pltpu.make_async_copy(s, d, in_sem.at[i]) for i, (s, d) in enumerate(loads)]
    barrier = pltpu.get_barrier_semaphore()

    def greet(cc, hh):
        pl.semaphore_signal(
            barrier, inc=1, device_id=(cc, hh), device_id_type=pl.DeviceIdType.MESH
        )

    def partner(level):
        bit = 2**level
        return c + bit - 2 * bit * ((c // bit) % 2)

    for j in range(4):
        @pl.when(jnp.logical_not(mixed & (x == j)))
        def _():
            greet(j * 8 + z * 2 + core, role_head)

    @pl.when(jnp.logical_not(mixed))
    def _():
        greet(partner(3), h)
        greet(partner(4), h)

    for dz in range(1, 4):
        greet(x * 8 + (z + dz) % 4 * 2 + yh, h)
        greet(c, (h + dz) % 4)
    greet(partner(0), h)

    @pl.when(z == 3)
    def _():
        greet((c + 2) % CTX, h)

    @pl.when(z == 0)
    def _():
        greet((c + CTX - 2) % CTX, h)

    for copy in loads:
        copy.start()

    loads[0].wait()
    loads[1].wait()
    for g in range(GROUPS):
        own = dot(kl[:, g * D : (g + 1) * D], vl[:, g * D : (g + 1) * D], 0, 0)
        state[g] = own
        fs[0, g] = own.astype(bf16)

    pl.semaphore_wait(
        barrier,
        jnp.where(mixed, 3, 6) + 7 + jnp.where((z == 0) | (z == 3), 1, 0),
    )

    def s1_copy(j, kv):
        src = (k_sh, v_sh)[kv].at[:, pl.ds(j * D, D)]
        dst = (kb, vb)[kv].at[z, x, pl.ds(yh * TOK, TOK), :]
        return src, dst

    def f_copy(level):
        return remote(
            fs.at[level], fr.at[level], fss.at[level], frs.at[level], partner(level), h
        )

    def fenwick(level):
        f_copy(level).wait_recv()
        got = fr[level]
        if level < 4:
            total = state[...] + got.astype(f32)
            state[...] = total
            fs[level + 1] = total.astype(bf16)
            f_copy(level + 1).start()

    f_copy(0).start()

    for j in range(4):
        for kv in range(2):
            src, dst = s1_copy(j, kv)
            local = mixed & (x == j)

            @pl.when(local)
            def _():
                pltpu.make_async_copy(src, dst, s1r.at[kv, j]).start()

            @pl.when(jnp.logical_not(local))
            def _():
                remote(
                    src, dst, s1s.at[kv, j], s1r.at[kv, x], j * 8 + z * 2 + core, role_head
                ).start()

    def q_copy(t):
        j = (x + 4 - t) % 4
        return (
            q_cross.at[:, pl.ds(j * GC, GC)], qb.at[x], qs.at[t], qr.at[x],
            j * 8 + z * 2 + core, role_head,
        )

    def q_start(t):
        src, dst, ssem, rsem, cc, hh = q_copy(t)
        if t == 0:
            @pl.when(mixed)
            def _():
                pltpu.make_async_copy(src, dst, rsem).start()

            @pl.when(jnp.logical_not(mixed))
            def _():
                remote(src, dst, ssem, rsem, cc, hh).start()
        else:
            remote(src, dst, ssem, rsem, cc, hh).start()

    def z_copy(kv, step):
        if step == 2:
            tile, to = ((z + 1) % 4, (z + 3) % 4) if kv == 0 else ((z + 3) % 4, (z + 1) % 4)
        else:
            tile, to = z, (z + 1 + 2 * step) % 4
        part = (kb, vb)[kv].at[tile, :, pl.ds(core * TOK, TOK), :]
        return remote(
            part, part, zs.at[kv, step], zr.at[kv, step], x * 8 + to * 2 + yh, h
        )

    def z_of(n):
        return (z + jnp.where(n == 1, 1, jnp.where(n == 2, 3, jnp.where(n == 3, 2, 0)))) % 4

    def b_copy(kv, n):
        part = (kb, vb)[kv].at[z_of(n), :, pl.ds(core * TOK, TOK), :]
        return remote(part, part, bs.at[kv, n], br.at[kv, n], c, h + 1 - 2 * core)

    def b_start(n):
        for kv in range(2):
            if n > 0:
                z_copy(kv, (1, 0, 2)[n - 1]).wait_recv()
            b_copy(kv, n).start()
        if n in (1, 2):
            z_copy(n - 1, 2).start()

    def b_wait(n):
        for kv in range(2):
            b_copy(kv, n).wait_recv()

    def own_chunk():
        for kv in range(2):
            for j in range(4):
                part = (kb, vb)[kv].at[z, j, pl.ds(core * TOK, TOK), :]
                remote(part, part, s1s.at[kv, 0], s1r.at[kv, j], c, h).wait_recv()
            for step in (0, 1):
                z_copy(kv, step).start()
        b_start(0)

    def w_copy(kv):
        return remote(
            (k_win, v_win)[kv], (wk, wv)[kv].at[0], ws.at[kv, 0], wr.at[kv, 0], c + 2, h
        )

    def w_start():
        for kv in range(2):
            @pl.when(c + 2 < CTX)
            def _():
                w_copy(kv).start()

    def y_copy(kv, slot):
        ref = (wk, wv)[kv]
        return remote(ref.at[slot], ref.at[1], ws.at[kv, 1], wr.at[kv, 1], partner(0), h)

    def w_arrive():
        for kv in range(2):
            ref = (wk, wv)[kv]

            @pl.when(c >= 2)
            def _():
                w_copy(kv).wait_recv()

            @pl.when(c < 2)
            def _():
                ref[0] = jnp.zeros((TOK, GROUPS * D), bf16)

            @pl.when(yh == 1)
            def _():
                y_copy(kv, 0).start()

    w_start()
    q_start(0)

    hot = (lax.broadcasted_iota(jnp.int32, (64, TOK), 0) == index[...]).astype(f32)
    lw[...] = dot(hot, table[...].reshape(LEVELS * HEADS, 64), 0, 1, lax.Precision.HIGHEST)

    loads[2].wait()
    rows = lax.broadcasted_iota(jnp.int32, (TOK, TOK), 0)
    cols = lax.broadcasted_iota(jnp.int32, (TOK, TOK), 1)
    causal = rows >= cols
    for g in range(GROUPS):
        for r in range(PER):
            hd = g * PER + r
            s = dot(ql[:, hd * D : (hd + 1) * D], kl[:, g * D : (g + 1) * D], 1, 1)
            s = jnp.where(causal, s * (D * TOK) ** -0.5, 0.0).astype(bf16)
            comb[:, hd * D : (hd + 1) * D] = lw[:, hd : hd + 1] * dot(
                s, vl[:, g * D : (g + 1) * D], 1, 0
            )

    fenwick(0)
    fenwick(1)
    own_chunk()
    for t in range(1, 4):
        q_start(t)
    for i in (3, 4, 5):
        loads[i].wait()

    step_row = lax.broadcasted_iota(jnp.int32, (TOK, 2 * TOK), 0) + core * TOK
    step_col = lax.broadcasted_iota(jnp.int32, (TOK, 2 * TOK), 1)
    step_mask = step_col <= step_row

    def attend(blk, chunk, parts, first):
        size = parts * 2 * TOK
        kk = kb[chunk, :parts].reshape(size, D)
        vv = vb[chunk, :parts].reshape(size, D)
        vv = jnp.concatenate([vv, jnp.ones((size, D), bf16)], axis=1)

        def scores(r):
            return dot(qb[blk, :, r * D : (r + 1) * D], kk, 1, 1)

        nxt = scores(0)
        for r in range(PER):
            s = nxt
            if r + 1 < PER:
                nxt = scores(r + 1)
            sl = pl.ds(r * TOK, TOK)
            if first:
                last = jnp.where(step_mask, s[:, size - 2 * TOK :], NEG)
                s = last if parts == 1 else jnp.concatenate([s[:, : size - 2 * TOK], last], axis=1)
                new = jnp.max(s, axis=1, keepdims=True)
            else:
                old = mx[blk, sl, :][:, :1]
                new = jnp.maximum(old, jnp.max(s, axis=1, keepdims=True))
            p = jnp.exp2(s * EXP2_SCALE - new * EXP2_SCALE).astype(bf16)
            o = dot(p, vv, 1, 0)
            if not first:
                o += acc[blk, sl, :] * jnp.exp2((old - new) * EXP2_SCALE)
            acc[blk, sl, :] = o
            mx[blk, sl, :] = jnp.broadcast_to(new, (TOK, D))

    def r_copy(blk):
        return remote(
            ob.at[blk], cr.at[x], rs.at[blk], rr.at[x],
            blk * 8 + z * 2 + core, role_head,
        )

    def send_back(blk):
        for r in range(PER):
            sl = pl.ds(r * TOK, TOK)
            ob[blk, :, r * D : (r + 1) * D] = (acc[blk, sl, :D] / acc[blk, sl, D:]).astype(bf16)
        local = mixed & (x == blk)

        @pl.when(local)
        def _():
            pltpu.make_async_copy(ob.at[blk], cr.at[x], rr.at[x]).start()

        @pl.when(jnp.logical_not(local))
        def _():
            r_copy(blk).start()

    def w_y_start():
        for kv in range(2):
            @pl.when(yh == 0)
            def _():
                y_copy(kv, 2).start()

    events = {
        0: [lambda: b_wait(0)],
        1: [lambda: fenwick(2)],
        2: [w_y_start],
        3: [w_arrive],
        4: [lambda: b_start(1), lambda: b_wait(1)],
        5: [lambda: fenwick(3)],
        6: [lambda: b_start(2)],
        8: [lambda: b_wait(2)],
        9: [lambda: fenwick(4)],
        10: [lambda: b_start(3)],
        12: [lambda: b_wait(3)],
    }

    def step(i, carry):
        n = i // 4
        chunk = z_of(n)
        blk = (x + i + jnp.where(n == 3, 1, 0)) % 4
        for at, todo in events.items():
            @pl.when(i == at)
            def _():
                for do in todo:
                    do()

        @pl.when(n == 0)
        def _():
            remote(
                q_cross.at[:, pl.ds(0, GC)], qb.at[blk], qs.at[0], qr.at[blk], c, h
            ).wait_recv()
            for j in range(4):
                @pl.when(blk == j)
                def _():
                    attend(blk, chunk, j + 1, True)

        @pl.when(n > 0)
        def _():
            parts = blk + jnp.where(chunk < z, 1, 0)
            for j in range(1, 5):
                @pl.when(parts == j)
                def _():
                    attend(blk, chunk, j, False)

        @pl.when(n == 3)
        def _():
            send_back(blk)

        return carry

    lax.fori_loop(0, 16, step, 0)

    for level in range(5):
        scale = jnp.where((c // 2**level) % 2 == 1, (D * TOK * 2**level) ** -0.5, 0.0)
        for g in range(GROUPS):
            bucket = fr[level, g]
            for r in range(PER):
                hd = g * PER + r
                term = dot(ql[:, hd * D : (hd + 1) * D], bucket, 1, 0)
                at = (level + 1) * HEADS + hd
                comb[:, hd * D : (hd + 1) * D] += (lw[:, at : at + 1] * scale) * term

    for kv in range(2):
        y_copy(kv, 0).wait_recv()

    far = 3 * TOK
    row = lax.broadcasted_iota(jnp.int32, (TOK, far), 0) + 2 * TOK
    col = lax.broadcasted_iota(jnp.int32, (TOK, far), 1)
    band = (col <= row) & (col > row - W) & (col >= (2 - c) * TOK)
    ones = jnp.ones((far, D), bf16)

    def window_group(g):
        kk = wk[:, :, g * D : (g + 1) * D].reshape(far, D)
        vv = jnp.concatenate([wv[:, :, g * D : (g + 1) * D].reshape(far, D), ones], axis=1)

        def scores(r):
            hd = g * PER + r
            return dot(qw[:, hd * D : (hd + 1) * D], kk, 1, 1)

        nxt = scores(0)
        for r in range(PER):
            s = nxt
            if r + 1 < PER:
                nxt = scores(r + 1)
            hd = g * PER + r
            s = jnp.where(band, s, NEG)
            top = jnp.max(s, axis=1, keepdims=True)
            p = jnp.exp2(s * EXP2_SCALE - top * EXP2_SCALE).astype(bf16)
            o = dot(p, vv, 1, 0)
            comb[:, hd * D : (hd + 1) * D] += o[:, :D] / o[:, D:]

    for g in range(GROUPS):
        window_group(g)


    square = jnp.zeros((TOK, D), f32)
    for j in range(4):
        remote(ob.at[j], cr.at[j], rs.at[j], rr.at[j], c, h).wait_recv()
        for r in range(PER):
            hd = j * PER + r
            at = slice(hd * D, (hd + 1) * D)
            v = (comb[:, at] + cr[j, :, r * D : (r + 1) * D].astype(f32)) * gain[hd]
            comb[:, at] = v
            square += v * v
    hs[...] = dot(jnp.ones((8, D), f32), square, 1, 1, lax.Precision.HIGHEST)
    for d in range(1, 4):
        remote(hs, hr.at[d - 1], hss.at[d - 1], hrs.at[d - 1], c, (h + d) % 4).start()
    total = hs[...]
    for d in range(1, 4):
        remote(hs, hr.at[d - 1], hss.at[d - 1], hrs.at[d - 1], c, (h + d) % 4).wait_recv()
        total = total + hr[d - 1]
    norm = lax.rsqrt(total / (4 * HEADS * D) + 1e-6).T[:, :1]
    for hd in range(HEADS):
        at = slice(hd * D, (hd + 1) * D)
        out[:, at] = (comb[:, at] * norm).astype(bf16)

    for j in range(4):
        local = mixed & (x == j)

        @pl.when(jnp.logical_not(local))
        def _():
            for kv in range(2):
                src, dst = s1_copy(j, kv)
                remote(src, dst, s1s.at[kv, j], s1r.at[kv, x], c, h).wait_send()
            r_copy(j).wait_send()
        for kv in range(2):
            b_copy(kv, j).wait_send()
    for kv in range(2):
        for n in range(3):
            z_copy(kv, n).wait_send()

    @pl.when(jnp.logical_not(mixed))
    def _():
        remote(*q_copy(0)).wait_send()

    for t in range(1, 4):
        remote(*q_copy(t)).wait_send()
    for kv in range(2):
        y_copy(kv, 0).wait_send()

        @pl.when(c + 2 < CTX)
        def _():
            w_copy(kv).wait_send()
    for level in range(5):
        f_copy(level).wait_send()
    for d in range(1, 4):
        remote(hs, hr.at[d - 1], hss.at[d - 1], hrs.at[d - 1], c, h).wait_send()


def per_device(
    q_win, k_win, v_win, q_lin, k_lin, v_lin, level_table, level_index, q_cross, k_shared,
    v_shared, head_gain,
):
    dma = pltpu.SemaphoreType.DMA
    whole = pl.BlockSpec(memory_space=pl.ANY)
    vmem = pl.BlockSpec(memory_space=pltpu.VMEM)
    smem = pl.BlockSpec(memory_space=pltpu.SMEM)
    kv = GROUPS * D
    return pl.pallas_call(
        kernel,
        out_shape=jax.ShapeDtypeStruct((TOK, HEADS * D), bf16),
        in_specs=[whole] * 6 + [vmem, vmem] + [whole] * 3 + [smem],
        out_specs=vmem,
        scratch_shapes=[
            pltpu.VMEM((TOK, HEADS * D), bf16),
            pltpu.VMEM((TOK, kv), bf16),
            pltpu.VMEM((TOK, kv), bf16),
            pltpu.VMEM((TOK, HEADS * D), bf16),
            pltpu.VMEM((3, TOK, kv), bf16),
            pltpu.VMEM((3, TOK, kv), bf16),
            pltpu.VMEM((4, TOK, GC), bf16),
            pltpu.VMEM((4, 4, 2 * TOK, D), bf16),
            pltpu.VMEM((4, 4, 2 * TOK, D), bf16),
            pltpu.VMEM((4, TOK, GC), bf16),
            pltpu.VMEM((4, TOK, GC), bf16),
            pltpu.VMEM((4, PER * TOK, 2 * D), f32),
            pltpu.VMEM((4, PER * TOK, D), f32),
            pltpu.VMEM((TOK, HEADS * D), f32),
            pltpu.VMEM((TOK, LEVELS * HEADS), f32),
            pltpu.VMEM((GROUPS, D, D), f32),
            pltpu.VMEM((5, GROUPS, D, D), bf16),
            pltpu.VMEM((5, GROUPS, D, D), bf16),
            pltpu.VMEM((8, TOK), f32),
            pltpu.VMEM((3, 8, TOK), f32),
            dma((6,)),
            dma((2, 4)), dma((2, 4)),
            dma((2, 2)), dma((2, 2)),
            dma((4,)), dma((4,)),
            dma((5,)), dma((5,)),
            dma((2, 3)), dma((2, 3)),
            dma((2, 4)), dma((2, 4)),
            dma((4,)), dma((4,)),
            dma((3,)), dma((3,)),
        ],
        compiler_params=pltpu.CompilerParams(
            collective_id=0, has_side_effects=True, vmem_limit_bytes=56 * 2**20
        ),
        name="hybrid_attention",
    )(
        q_win, k_win, v_win, q_lin, k_lin, v_lin,
        level_table.transpose(2, 1, 0), level_index.reshape(1, -1),
        q_cross, k_shared, v_shared, head_gain,
    )


def solution(mesh):
    return jax.shard_map(
        per_device,
        mesh=mesh,
        in_specs=(
            P("ctx", "head"),
            P("ctx", "head"),
            P("ctx", "head"),
            P("ctx", "head"),
            P("ctx", "head"),
            P("ctx", "head"),
            P(None, "head", None),
            P("ctx"),
            P("ctx", "head"),
            P("ctx", "head"),
            P("ctx", "head"),
            P("head"),
        ),
        out_specs=P("ctx", "head"),
        check_vma=False,
    )
```

```python
import jax
import jax.numpy as jnp
from jax import lax
from jax.experimental import pallas as pl
from jax.experimental.pallas import tpu as pltpu
from jax.sharding import PartitionSpec as P

bf16 = jnp.bfloat16
f32 = jnp.float32
TOK = 256
D = 128
HEADS = 16
GROUPS = 4
PER = 4
GC = PER * D
LEVELS = 6
W = 512
CTX = 32
NEG = -1e30
EXP2_SCALE = D**-0.5 * 1.4426950408889634


def dot(a, b, ca, cb, precision=None):
    return lax.dot_general(
        a, b, (((ca,), (cb,)), ((), ())), preferred_element_type=f32, precision=precision
    )


def kernel(
    q_win, k_win, v_win, q_lin, k_lin, v_lin, table, index, q_cross, k_sh, v_sh, gain,
    out,
    ql, kl, vl, qw, wk, wv, qb, kb, vb, ob, cr, acc, mx, comb, lw,
    state, fs, fr, hs, hr,
    in_sem, s1s, s1r, ws, wr, qs, qr, fss, frs, zs, zr, bs, br, rs, rr, hss, hrs,
):
    c = lax.axis_index("ctx")
    h = lax.axis_index("head")
    x, z, yh = c // 8, (c // 2) % 4, c % 2
    ylo, core = h // 2, h % 2
    role_head = ylo * 2 + yh
    mixed = core == yh

    def remote(src, dst, ssem, rsem, cc, hh):
        return pltpu.make_async_remote_copy(
            src_ref=src, dst_ref=dst, send_sem=ssem, recv_sem=rsem,
            device_id=(cc, hh), device_id_type=pl.DeviceIdType.MESH,
        )

    loads = [
        (k_lin, kl), (v_lin, vl), (q_lin, ql), (k_win, wk.at[2]), (v_win, wv.at[2]), (q_win, qw),
    ]
    loads = [pltpu.make_async_copy(s, d, in_sem.at[i]) for i, (s, d) in enumerate(loads)]
    barrier = pltpu.get_barrier_semaphore()

    def greet(cc, hh):
        pl.semaphore_signal(
            barrier, inc=1, device_id=(cc, hh), device_id_type=pl.DeviceIdType.MESH
        )

    def partner(level):
        bit = 2**level
        return c + bit - 2 * bit * ((c // bit) % 2)

    for j in range(4):
        @pl.when(jnp.logical_not(mixed & (x == j)))
        def _():
            greet(j * 8 + z * 2 + core, role_head)

    @pl.when(jnp.logical_not(mixed))
    def _():
        greet(partner(3), h)
        greet(partner(4), h)

    for dz in range(1, 4):
        greet(x * 8 + (z + dz) % 4 * 2 + yh, h)
        greet(c, (h + dz) % 4)
    greet(partner(0), h)

    @pl.when(z == 3)
    def _():
        greet((c + 2) % CTX, h)

    @pl.when(z == 0)
    def _():
        greet((c + CTX - 2) % CTX, h)

    for copy in loads:
        copy.start()

    loads[0].wait()
    loads[1].wait()
    for g in range(GROUPS):
        own = dot(kl[:, g * D : (g + 1) * D], vl[:, g * D : (g + 1) * D], 0, 0)
        state[g] = own
        fs[0, g] = own.astype(bf16)

    pl.semaphore_wait(
        barrier,
        jnp.where(mixed, 3, 6) + 7 + jnp.where((z == 0) | (z == 3), 1, 0),
    )

    def s1_copy(j, kv):
        src = (k_sh, v_sh)[kv].at[:, pl.ds(j * D, D)]
        dst = (kb, vb)[kv].at[z, x, pl.ds(yh * TOK, TOK), :]
        return src, dst

    def f_copy(level):
        return remote(
            fs.at[level], fr.at[level], fss.at[level], frs.at[level], partner(level), h
        )

    def fenwick(level):
        f_copy(level).wait_recv()
        got = fr[level]
        if level < 4:
            total = state[...] + got.astype(f32)
            state[...] = total
            fs[level + 1] = total.astype(bf16)
            f_copy(level + 1).start()

    f_copy(0).start()

    for j in range(4):
        for kv in range(2):
            src, dst = s1_copy(j, kv)
            local = mixed & (x == j)

            @pl.when(local)
            def _():
                pltpu.make_async_copy(src, dst, s1r.at[kv, j]).start()

            @pl.when(jnp.logical_not(local))
            def _():
                remote(
                    src, dst, s1s.at[kv, j], s1r.at[kv, x], j * 8 + z * 2 + core, role_head
                ).start()

    def q_copy(t):
        j = (x + 4 - t) % 4
        return (
            q_cross.at[:, pl.ds(j * GC, GC)], qb.at[x], qs.at[t], qr.at[x],
            j * 8 + z * 2 + core, role_head,
        )

    def q_start(t):
        src, dst, ssem, rsem, cc, hh = q_copy(t)
        if t == 0:
            @pl.when(mixed)
            def _():
                pltpu.make_async_copy(src, dst, rsem).start()

            @pl.when(jnp.logical_not(mixed))
            def _():
                remote(src, dst, ssem, rsem, cc, hh).start()
        else:
            remote(src, dst, ssem, rsem, cc, hh).start()

    def z_copy(kv, step):
        if step == 2:
            tile, to = ((z + 1) % 4, (z + 3) % 4) if kv == 0 else ((z + 3) % 4, (z + 1) % 4)
        else:
            tile, to = z, (z + 1 + 2 * step) % 4
        part = (kb, vb)[kv].at[tile, :, pl.ds(core * TOK, TOK), :]
        return remote(
            part, part, zs.at[kv, step], zr.at[kv, step], x * 8 + to * 2 + yh, h
        )

    def z_of(n):
        return (z + jnp.where(n == 1, 1, jnp.where(n == 2, 3, jnp.where(n == 3, 2, 0)))) % 4

    def b_copy(kv, n):
        part = (kb, vb)[kv].at[z_of(n), :, pl.ds(core * TOK, TOK), :]
        return remote(part, part, bs.at[kv, n], br.at[kv, n], c, h + 1 - 2 * core)

    def b_start(n):
        for kv in range(2):
            if n > 0:
                z_copy(kv, (1, 0, 2)[n - 1]).wait_recv()
            b_copy(kv, n).start()
        if n in (1, 2):
            z_copy(n - 1, 2).start()

    def b_wait(n):
        for kv in range(2):
            b_copy(kv, n).wait_recv()

    def own_chunk():
        for kv in range(2):
            for j in range(4):
                part = (kb, vb)[kv].at[z, j, pl.ds(core * TOK, TOK), :]
                remote(part, part, s1s.at[kv, 0], s1r.at[kv, j], c, h).wait_recv()
            for step in (0, 1):
                z_copy(kv, step).start()
        b_start(0)

    def w_copy(kv):
        return remote(
            (k_win, v_win)[kv], (wk, wv)[kv].at[0], ws.at[kv, 0], wr.at[kv, 0], c + 2, h
        )

    def w_start():
        for kv in range(2):
            @pl.when(c + 2 < CTX)
            def _():
                w_copy(kv).start()

    def y_copy(kv, slot):
        ref = (wk, wv)[kv]
        return remote(ref.at[slot], ref.at[1], ws.at[kv, 1], wr.at[kv, 1], partner(0), h)

    def w_arrive():
        for kv in range(2):
            ref = (wk, wv)[kv]

            @pl.when(c >= 2)
            def _():
                w_copy(kv).wait_recv()

            @pl.when(c < 2)
            def _():
                ref[0] = jnp.zeros((TOK, GROUPS * D), bf16)

            @pl.when(yh == 1)
            def _():
                y_copy(kv, 0).start()

    w_start()
    q_start(0)

    hot = (lax.broadcasted_iota(jnp.int32, (64, TOK), 0) == index[...]).astype(f32)
    lw[...] = dot(hot, table[...].reshape(LEVELS * HEADS, 64), 0, 1, lax.Precision.HIGHEST)

    loads[2].wait()
    rows = lax.broadcasted_iota(jnp.int32, (TOK, TOK), 0)
    cols = lax.broadcasted_iota(jnp.int32, (TOK, TOK), 1)
    causal = rows >= cols
    for g in range(GROUPS):
        for r in range(PER):
            hd = g * PER + r
            s = dot(ql[:, hd * D : (hd + 1) * D], kl[:, g * D : (g + 1) * D], 1, 1)
            s = jnp.where(causal, s * (D * TOK) ** -0.5, 0.0).astype(bf16)
            comb[:, hd * D : (hd + 1) * D] = lw[:, hd : hd + 1] * dot(
                s, vl[:, g * D : (g + 1) * D], 1, 0
            )

    fenwick(0)
    own_chunk()
    fenwick(1)
    for t in range(1, 4):
        q_start(t)
    for i in (3, 4, 5):
        loads[i].wait()

    step_row = lax.broadcasted_iota(jnp.int32, (TOK, 2 * TOK), 0) + core * TOK
    step_col = lax.broadcasted_iota(jnp.int32, (TOK, 2 * TOK), 1)
    step_mask = step_col <= step_row

    def attend(blk, chunk, parts, first):
        size = parts * 2 * TOK
        kk = kb[chunk, :parts].reshape(size, D)
        vv = vb[chunk, :parts].reshape(size, D)
        vv = jnp.concatenate([vv, jnp.ones((size, D), bf16)], axis=1)

        def scores(r):
            return dot(qb[blk, :, r * D : (r + 1) * D], kk, 1, 1)

        nxt = scores(0)
        for r in range(PER):
            s = nxt
            if r + 1 < PER:
                nxt = scores(r + 1)
            sl = pl.ds(r * TOK, TOK)
            if first:
                last = jnp.where(step_mask, s[:, size - 2 * TOK :], NEG)
                s = last if parts == 1 else jnp.concatenate([s[:, : size - 2 * TOK], last], axis=1)
                new = jnp.max(s, axis=1, keepdims=True)
            else:
                old = mx[blk, sl, :][:, :1]
                new = jnp.maximum(old, jnp.max(s, axis=1, keepdims=True))
            p = jnp.exp2(s * EXP2_SCALE - new * EXP2_SCALE).astype(bf16)
            o = dot(p, vv, 1, 0)
            if not first:
                o += acc[blk, sl, :] * jnp.exp2((old - new) * EXP2_SCALE)
            acc[blk, sl, :] = o
            mx[blk, sl, :] = jnp.broadcast_to(new, (TOK, D))

    def r_copy(blk):
        return remote(
            ob.at[blk], cr.at[x], rs.at[blk], rr.at[x],
            blk * 8 + z * 2 + core, role_head,
        )

    def send_back(blk):
        for r in range(PER):
            sl = pl.ds(r * TOK, TOK)
            ob[blk, :, r * D : (r + 1) * D] = (acc[blk, sl, :D] / acc[blk, sl, D:]).astype(bf16)
        local = mixed & (x == blk)

        @pl.when(local)
        def _():
            pltpu.make_async_copy(ob.at[blk], cr.at[x], rr.at[x]).start()

        @pl.when(jnp.logical_not(local))
        def _():
            r_copy(blk).start()

    def w_y_start():
        for kv in range(2):
            @pl.when(yh == 0)
            def _():
                y_copy(kv, 2).start()

    events = {
        0: [lambda: b_wait(0)],
        1: [lambda: fenwick(2)],
        2: [w_y_start],
        3: [w_arrive],
        4: [lambda: b_start(1), lambda: b_wait(1)],
        5: [lambda: fenwick(3)],
        6: [lambda: b_start(2)],
        8: [lambda: b_wait(2)],
        9: [lambda: fenwick(4)],
        10: [lambda: b_start(3)],
        12: [lambda: b_wait(3)],
    }

    def step(i, carry):
        n = i // 4
        chunk = z_of(n)
        blk = (x + i + jnp.where(n == 3, 1, 0)) % 4
        for at, todo in events.items():
            @pl.when(i == at)
            def _():
                for do in todo:
                    do()

        @pl.when(n == 0)
        def _():
            remote(
                q_cross.at[:, pl.ds(0, GC)], qb.at[blk], qs.at[0], qr.at[blk], c, h
            ).wait_recv()
            for j in range(4):
                @pl.when(blk == j)
                def _():
                    attend(blk, chunk, j + 1, True)

        @pl.when(n > 0)
        def _():
            parts = blk + jnp.where(chunk < z, 1, 0)
            for j in range(1, 5):
                @pl.when(parts == j)
                def _():
                    attend(blk, chunk, j, False)

        @pl.when(n == 3)
        def _():
            send_back(blk)

        return carry

    lax.fori_loop(0, 16, step, 0)

    for level in range(5):
        scale = jnp.where((c // 2**level) % 2 == 1, (D * TOK * 2**level) ** -0.5, 0.0)
        for g in range(GROUPS):
            bucket = fr[level, g]
            for r in range(PER):
                hd = g * PER + r
                term = dot(ql[:, hd * D : (hd + 1) * D], bucket, 1, 0)
                at = (level + 1) * HEADS + hd
                comb[:, hd * D : (hd + 1) * D] += (lw[:, at : at + 1] * scale) * term

    for kv in range(2):
        y_copy(kv, 0).wait_recv()

    far = 3 * TOK
    row = lax.broadcasted_iota(jnp.int32, (TOK, far), 0) + 2 * TOK
    col = lax.broadcasted_iota(jnp.int32, (TOK, far), 1)
    band = (col <= row) & (col > row - W) & (col >= (2 - c) * TOK)
    ones = jnp.ones((far, D), bf16)

    def window_group(g):
        kk = wk[:, :, g * D : (g + 1) * D].reshape(far, D)
        vv = jnp.concatenate([wv[:, :, g * D : (g + 1) * D].reshape(far, D), ones], axis=1)

        def scores(r):
            hd = g * PER + r
            return dot(qw[:, hd * D : (hd + 1) * D], kk, 1, 1)

        nxt = scores(0)
        for r in range(PER):
            s = nxt
            if r + 1 < PER:
                nxt = scores(r + 1)
            hd = g * PER + r
            s = jnp.where(band, s, NEG)
            top = jnp.max(s, axis=1, keepdims=True)
            p = jnp.exp2(s * EXP2_SCALE - top * EXP2_SCALE).astype(bf16)
            o = dot(p, vv, 1, 0)
            comb[:, hd * D : (hd + 1) * D] += o[:, :D] / o[:, D:]

    for g in range(GROUPS):
        window_group(g)


    square = jnp.zeros((TOK, D), f32)
    for j in range(4):
        remote(ob.at[j], cr.at[j], rs.at[j], rr.at[j], c, h).wait_recv()
        for r in range(PER):
            hd = j * PER + r
            at = slice(hd * D, (hd + 1) * D)
            v = (comb[:, at] + cr[j, :, r * D : (r + 1) * D].astype(f32)) * gain[hd]
            comb[:, at] = v
            square += v * v
    hs[...] = dot(jnp.ones((8, D), f32), square, 1, 1, lax.Precision.HIGHEST)
    for d in range(1, 4):
        remote(hs, hr.at[d - 1], hss.at[d - 1], hrs.at[d - 1], c, (h + d) % 4).start()
    total = hs[...]
    for d in range(1, 4):
        remote(hs, hr.at[d - 1], hss.at[d - 1], hrs.at[d - 1], c, (h + d) % 4).wait_recv()
        total = total + hr[d - 1]
    norm = lax.rsqrt(total / (4 * HEADS * D) + 1e-6).T[:, :1]
    for hd in range(HEADS):
        at = slice(hd * D, (hd + 1) * D)
        out[:, at] = (comb[:, at] * norm).astype(bf16)

    for j in range(4):
        local = mixed & (x == j)

        @pl.when(jnp.logical_not(local))
        def _():
            for kv in range(2):
                src, dst = s1_copy(j, kv)
                remote(src, dst, s1s.at[kv, j], s1r.at[kv, x], c, h).wait_send()
            r_copy(j).wait_send()
        for kv in range(2):
            b_copy(kv, j).wait_send()
    for kv in range(2):
        for n in range(3):
            z_copy(kv, n).wait_send()

    @pl.when(jnp.logical_not(mixed))
    def _():
        remote(*q_copy(0)).wait_send()

    for t in range(1, 4):
        remote(*q_copy(t)).wait_send()
    for kv in range(2):
        y_copy(kv, 0).wait_send()

        @pl.when(c + 2 < CTX)
        def _():
            w_copy(kv).wait_send()
    for level in range(5):
        f_copy(level).wait_send()
    for d in range(1, 4):
        remote(hs, hr.at[d - 1], hss.at[d - 1], hrs.at[d - 1], c, h).wait_send()


def per_device(
    q_win, k_win, v_win, q_lin, k_lin, v_lin, level_table, level_index, q_cross, k_shared,
    v_shared, head_gain,
):
    dma = pltpu.SemaphoreType.DMA
    whole = pl.BlockSpec(memory_space=pl.ANY)
    vmem = pl.BlockSpec(memory_space=pltpu.VMEM)
    smem = pl.BlockSpec(memory_space=pltpu.SMEM)
    kv = GROUPS * D
    return pl.pallas_call(
        kernel,
        out_shape=jax.ShapeDtypeStruct((TOK, HEADS * D), bf16),
        in_specs=[whole] * 6 + [vmem, vmem] + [whole] * 3 + [smem],
        out_specs=vmem,
        scratch_shapes=[
            pltpu.VMEM((TOK, HEADS * D), bf16),
            pltpu.VMEM((TOK, kv), bf16),
            pltpu.VMEM((TOK, kv), bf16),
            pltpu.VMEM((TOK, HEADS * D), bf16),
            pltpu.VMEM((3, TOK, kv), bf16),
            pltpu.VMEM((3, TOK, kv), bf16),
            pltpu.VMEM((4, TOK, GC), bf16),
            pltpu.VMEM((4, 4, 2 * TOK, D), bf16),
            pltpu.VMEM((4, 4, 2 * TOK, D), bf16),
            pltpu.VMEM((4, TOK, GC), bf16),
            pltpu.VMEM((4, TOK, GC), bf16),
            pltpu.VMEM((4, PER * TOK, 2 * D), f32),
            pltpu.VMEM((4, PER * TOK, D), f32),
            pltpu.VMEM((TOK, HEADS * D), f32),
            pltpu.VMEM((TOK, LEVELS * HEADS), f32),
            pltpu.VMEM((GROUPS, D, D), f32),
            pltpu.VMEM((5, GROUPS, D, D), bf16),
            pltpu.VMEM((5, GROUPS, D, D), bf16),
            pltpu.VMEM((8, TOK), f32),
            pltpu.VMEM((3, 8, TOK), f32),
            dma((6,)),
            dma((2, 4)), dma((2, 4)),
            dma((2, 2)), dma((2, 2)),
            dma((4,)), dma((4,)),
            dma((5,)), dma((5,)),
            dma((2, 3)), dma((2, 3)),
            dma((2, 4)), dma((2, 4)),
            dma((4,)), dma((4,)),
            dma((3,)), dma((3,)),
        ],
        compiler_params=pltpu.CompilerParams(
            collective_id=0, has_side_effects=True, vmem_limit_bytes=56 * 2**20
        ),
        name="hybrid_attention",
    )(
        q_win, k_win, v_win, q_lin, k_lin, v_lin,
        level_table.transpose(2, 1, 0), level_index.reshape(1, -1),
        q_cross, k_shared, v_shared, head_gain,
    )


def solution(mesh):
    return jax.shard_map(
        per_device,
        mesh=mesh,
        in_specs=(
            P("ctx", "head"),
            P("ctx", "head"),
            P("ctx", "head"),
            P("ctx", "head"),
            P("ctx", "head"),
            P("ctx", "head"),
            P(None, "head", None),
            P("ctx"),
            P("ctx", "head"),
            P("ctx", "head"),
            P("ctx", "head"),
            P("head"),
        ),
        out_specs=P("ctx", "head"),
        check_vma=False,
    )
```
